256 devices in a mesh: region: 64 (over z, y, core), mp: 4 (over x).
Axes of the slice: x: 4, y: 4, z: 8, core: 2. Of those that a mesh axis runs over, the one named last changes fastest.
Arguments:
- grid_state: bfloat16 [524288, 268], P(('region', 'mp')), may hold values from -6 to 6
- targets: int32 [524288], P(('region', 'mp')), may hold values from 0 to 40959, as said below
- neighbours: int32 [40960, 32], P('region'), may hold values from 0 to 40959, as said below
- w_in: bfloat16 [268, 512], replicated, may hold values from -0.375 to 0.375
- b_in: float32 [512], replicated, may hold values from -0.5 to 0.5
- mesh_gain: float32 [512], replicated, may hold values from 1 to 2
- w_qkv: bfloat16 [3, 512, 512], P(None, None, 'mp'), may hold values from -0.25 to 0.25
- w_out: bfloat16 [512, 512], P('mp'), may hold values from -0.25 to 0.25
- w_dec: bfloat16 [512, 512], replicated, may hold values from -0.25 to 0.25
- w_head: bfloat16 [512, 84], replicated, may hold values from -0.25 to 0.25
Outputs:
- denoised: float32 [524288, 84], P(('region', 'mp'))
The draws below stay inside these ranges and needn't reach their ends.
Inputs may be any that keep to these rules, and one draw needn't show every extreme that they name: `targets`: the mesh node of a grid point of region r (rows r * 2048 * 4 onward) belongs to region r or r + 1 cyclically; region r owns nodes r * 640 onward. `neighbours`: every neighbour of a node of region r belongs to region r - 1, r or r + 1 cyclically.
All inputs are finite; a program needn't handle non-finite values.
Results may differ from the reference program's by a relative error of at most 0.022.
Values may be sent and summed in bfloat16 or wider, within the bound.
A program may use at most 64 MiB of HBM per device.

```python
import jax
import jax.numpy as jnp
from jax import lax

D = 512
HEADS = 4
HEAD_WIDTH = 128
NBR = 32
C_IN = 268
C_OUT = 84
MESH_PER_REGION = 640
GRID_DEV = 2048
NMESH = 40960
GRID = 524288
N_REGION = 64
N_MP = 4


def route_targets(key):
    key = jax.random.fold_in(key, 11)
    first, second = jax.random.split(key)
    count = GRID_DEV * N_REGION * N_MP
    rows = jnp.arange(count, dtype=jnp.int32)
    region = rows // (GRID_DEV * N_MP)
    step = (jax.random.randint(first, (count,), 0, 4) == 0).astype(jnp.int32)
    local = jax.random.randint(second, (count,), 0, MESH_PER_REGION)
    return (jnp.mod(region + step, N_REGION) * MESH_PER_REGION + local).astype(jnp.int32)


def draw_targets(key, part):
    routed = route_targets(key)
    return routed


def draw_grid_state(key, part):
    routed = route_targets(key)
    key = jax.random.fold_in(key, 37)
    pattern_key, noise_key = jax.random.split(key, 2)
    count = GRID_DEV * N_REGION * N_MP
    pattern = jax.random.normal(pattern_key, (NMESH, C_IN), jnp.float32)
    noise = 0.6 * jax.random.normal(noise_key, (count, C_IN), jnp.float32)
    rows = jnp.clip(pattern[routed] + noise, -6.0, 6.0)
    return rows.astype(jnp.bfloat16)


def draw_neighbours(key, part):
    key = jax.random.fold_in(key, 23)
    first, second = jax.random.split(key)
    count = MESH_PER_REGION * N_REGION
    region = (jnp.arange(count, dtype=jnp.int32) // MESH_PER_REGION)[:, None]
    offset = jax.random.randint(first, (count, NBR), 0, 3) - 1
    local = jax.random.randint(second, (count, NBR), 0, MESH_PER_REGION)
    return (jnp.mod(region + offset, N_REGION) * MESH_PER_REGION + local).astype(jnp.int32)


def level_of(key, extent, cuts, low, largest):
    loudness, own = 1.0, jax.random.fold_in(key, 6)
    for axis_at, blocks in cuts:
        heights = jnp.exp(jax.random.uniform(jax.random.fold_in(own, axis_at), (blocks,), jnp.float32, low / len(cuts), largest / len(cuts)))
        loudness = loudness * jnp.repeat(heights, extent[axis_at] // blocks).reshape([-1 if axis == axis_at else 1 for axis in range(len(extent))])
    return loudness


def scatter_about(own_key, extent, scale, most, cuts=(), kind=jnp.bfloat16):
    result = jax.random.normal(own_key, extent, jnp.float32) * scale
    if len(cuts) > 0:
        result = level_of(own_key, extent, cuts, -0.22, 0.18) * result
    return jnp.clip(result, min=-most, max=most).astype(kind)


def setup_inputs(seed: int = 0) -> dict:
    key_of = jax.random.split(jax.random.key(seed), 11)
    grid_state = draw_grid_state(jax.random.fold_in(key_of[10], 71), 0)
    targets = draw_targets(jax.random.fold_in(key_of[10], 71), 0)
    neighbours = draw_neighbours(jax.random.fold_in(key_of[10], 71), 0)
    w_in = scatter_about(key_of[3], (C_IN, D), C_IN ** -0.5, 0.375)
    b_in = jnp.clip(jax.random.uniform(key_of[4], (D,), jnp.float32, -0.5, 0.5), -0.5, 0.5)
    mesh_gain = jnp.clip(jax.random.uniform(key_of[5], (D,), jnp.float32, 1.0, 2.0), 1.0, 2.0)
    w_qkv = scatter_about(key_of[6], (3, D, HEADS * HEAD_WIDTH), D ** -0.5, 0.25, ((2, 4),))
    w_out = scatter_about(key_of[7], (HEADS * HEAD_WIDTH, D), (HEADS * HEAD_WIDTH) ** -0.5, 0.25, ((0, 4),))
    w_dec = scatter_about(key_of[8], (D, D), D ** -0.5, 0.25)
    w_head = scatter_about(key_of[9], (D, C_OUT), D ** -0.5, 0.25)
    return {"grid_state": grid_state, "targets": targets, "neighbours": neighbours, "w_in": w_in, "b_in": b_in, "mesh_gain": mesh_gain, "w_qkv": w_qkv, "w_out": w_out, "w_dec": w_dec, "w_head": w_head}


def embed_rows(rows, w_in, b_in):
    return jax.nn.silu(jnp.dot(rows, w_in, preferred_element_type=jnp.float32) + b_in).astype(jnp.bfloat16)

def reference(grid_state, targets, neighbours, w_in, b_in, mesh_gain, w_qkv, w_out, w_dec, w_head):
    block = GRID_DEV * N_MP

    def encode(total, index):
        rows = lax.dynamic_slice_in_dim(grid_state, index * block, block, 0)
        where = lax.dynamic_slice_in_dim(targets, index * block, block, 0)
        embed = embed_rows(rows, w_in, b_in)
        return (total + jax.ops.segment_sum(embed.astype(jnp.float32), where, num_segments=NMESH), None)
    mesh_in, _ = lax.scan(encode, jnp.zeros((NMESH, D), jnp.float32), jnp.arange(N_REGION, dtype=jnp.int32))
    state = (mesh_in * lax.rsqrt(lax.optimization_barrier(jnp.mean(mesh_in * mesh_in, axis=-1, keepdims=True)) + 1e-05) * mesh_gain).astype(jnp.bfloat16)
    query = jnp.dot(state, w_qkv[0], preferred_element_type=jnp.float32).astype(jnp.bfloat16)
    keys = jnp.dot(state, w_qkv[1], preferred_element_type=jnp.float32).astype(jnp.bfloat16)
    values = jnp.dot(state, w_qkv[2], preferred_element_type=jnp.float32).astype(jnp.bfloat16)

    def attend(index):
        table = lax.dynamic_slice_in_dim(neighbours, index * MESH_PER_REGION, MESH_PER_REGION, 0)
        query_rows = lax.dynamic_slice_in_dim(query, index * MESH_PER_REGION, MESH_PER_REGION, 0)
        query_rows = query_rows.reshape(MESH_PER_REGION, HEADS, HEAD_WIDTH).astype(jnp.float32)
        nearby_key_rows = keys[table].reshape(MESH_PER_REGION, NBR, HEADS, HEAD_WIDTH).astype(jnp.float32)
        nearby_value_rows = values[table].reshape(MESH_PER_REGION, NBR, HEADS, HEAD_WIDTH).astype(jnp.float32)
        attention_logits = jnp.einsum('fkp,fekp->fke', query_rows, nearby_key_rows) / jnp.sqrt(jnp.float32(HEAD_WIDTH))
        attention_weight_table = jax.nn.softmax(attention_logits, axis=-1).astype(jnp.bfloat16)
        mixed_heads_output = jnp.einsum('wtc,wctb->wtb', attention_weight_table.astype(jnp.float32), nearby_value_rows)
        return mixed_heads_output.astype(jnp.bfloat16).reshape(MESH_PER_REGION, HEADS * HEAD_WIDTH)
    mixed_heads_output = lax.map(attend, jnp.arange(N_REGION, dtype=jnp.int32)).reshape(NMESH, HEADS * HEAD_WIDTH)
    mesh_out = (state.astype(jnp.float32) + jnp.dot(mixed_heads_output, w_out, preferred_element_type=jnp.float32)).astype(jnp.bfloat16)

    def decode_to_grid(index):
        rows = lax.dynamic_slice_in_dim(grid_state, index * block, block, 0)
        where = lax.dynamic_slice_in_dim(targets, index * block, block, 0)
        embed = embed_rows(rows, w_in, b_in)
        dec_in = (mesh_out[where].astype(jnp.float32) + embed.astype(jnp.float32)).astype(jnp.bfloat16)
        hidden = jax.nn.silu(jnp.dot(dec_in, w_dec, preferred_element_type=jnp.float32)).astype(jnp.bfloat16)
        return jnp.dot(hidden, w_head, preferred_element_type=jnp.float32)
    return lax.map(decode_to_grid, jnp.arange(N_REGION, dtype=jnp.int32)).reshape(GRID, C_OUT)
```

```python
import functools

import jax
import jax.numpy as jnp
from jax import lax
from jax.experimental import pallas as pl
from jax.experimental.pallas import tpu as pltpu
from jax.sharding import PartitionSpec as P

MESH = pl.DeviceIdType.MESH
BF16 = jnp.bfloat16
F32 = jnp.float32
LOG2_E = 1.4426950408889634
ABSENT = -1e30

NAMES = (
    *("wr", "wl", "w2r", "w2l", "ws0", "ws1", "ws2", "ws3"),
    *("or", "ol", "o2r", "o2l", "os0", "os1", "os2", "os3"),
    *("n0", "n1", "n2", "n3"),
    *("ar", "al", "br0", "br1", "bl0", "bl1"),
    *("sr", "sl", "s2r", "s2l"),
    *("su0", "su1", "su2", "su3", "su4", "sd0", "sd1", "sd2", "sd3", "sd4"),
    *("mr", "ml", "m2r", "m2l", "md0", "md1", "md2", "md3", "md4"),
)
INDEX = {name: i for i, name in enumerate(NAMES)}


def nt(a, b):
    return lax.dot_general(a, b, (((1,), (1,)), ((), ())), preferred_element_type=F32)


def nn(a, b):
    return jnp.dot(a, b, preferred_element_type=F32)


def silu(z):
    half = 0.5 * z
    return half + half * jnp.tanh(half)


def kernel(
    regions,
    x_hbm, targets_ref, nbr_ref, w_in_hbm, b_ref, gain_ref, wqkv_hbm, wo_hbm, wdec_hbm, whead_hbm,
    out_ref,
    x, w_in, w_in_t, b_t, wqkv, wo, wdec, wdec_t, whead,
    rel, slots, onehot, embed, e2, send_n, recv_n, part, ra, ra_l, ra_r, rb, rb_l, rb_r,
    st, qp, bias, mix, md, md_t,
    ssem, rsem, lsem,
):
    r = lax.axis_index("region")
    m = lax.axis_index("mp")
    mps = 4
    up = (lax.rem(r + 1, regions), m)
    down = (lax.rem(r + regions - 1, regions), m)
    right_m = lax.rem(m + 1, mps)
    left_m = lax.rem(m + mps - 1, mps)
    opp_m = lax.rem(m + 2, mps)
    right = (r, right_m)
    left = (r, left_m)
    core = lax.rem(r, 2)
    sibling = (r + 1 - 2 * core, m)

    channels, points = x.shape
    width = embed.shape[0]
    quarter = st.shape[0] // 12
    nodes = 4 * quarter
    half = quarter // 2
    neighbours = slots.shape[1]
    heads, head_width = wo.shape[0], wo.shape[1]
    block = min(256, points)
    blocks = points // block

    started = []

    def copy(name, src, dst, dev):
        i = INDEX[name]
        return pltpu.make_async_remote_copy(
            src_ref=src, dst_ref=dst, send_sem=ssem.at[i], recv_sem=rsem.at[i],
            device_id=dev, device_id_type=MESH,
        )

    def send(name, src, dst, dev):
        c = copy(name, src, dst, dev)
        c.start()
        started.append(c)

    def arrived(name, dst):
        copy(name, dst, dst, right).wait_recv()

    loads = {}
    for i, (name, src, dst) in enumerate((
        ("w_in", w_in_hbm, w_in), ("x", x_hbm, x), ("wqkv", wqkv_hbm, wqkv.at[m]),
        ("wo", wo_hbm, wo.at[m]), ("wdec", wdec_hbm, wdec), ("whead", whead_hbm, whead),
    )):
        loads[name] = pltpu.make_async_copy(src, dst, lsem.at[i])
        loads[name].start()

    barrier = pltpu.get_barrier_semaphore()
    for dev in (up, down, right, left):
        pl.semaphore_signal(barrier, inc=1, device_id=dev, device_id_type=MESH)

    here = r * nodes
    total = regions * nodes
    t = targets_ref[...] - here
    rel[...] = jnp.where(t < 0, t + total, t)
    b_t[...] = jnp.transpose(jnp.broadcast_to(b_ref[...], (128, width)))
    loads["w_in"].wait()
    w_in_t[...] = jnp.transpose(w_in[...].astype(F32)).astype(BF16)

    pl.semaphore_wait(barrier, 4)

    hq = width // 2
    ho = head_width // 2

    def qkv_part(h, start, size):
        return wqkv.at[h, :, pl.ds(pl.multiple_of(start, 16), size), :]

    def wo_part(h, start, size):
        return wo.at[h, pl.ds(pl.multiple_of(start, 16), size), :]

    q0, o0 = core * hq, core * ho
    loads["wqkv"].wait()
    loads["wo"].wait()
    for name, dev in (("r", right), ("l", left)):
        send("w" + name, qkv_part(m, q0, hq), qkv_part(m, q0, hq), dev)
        send("o" + name, wo_part(m, o0, ho), wo_part(m, o0, ho), dev)

    loads["x"].wait()

    def embed_block(i, _):
        cols = pl.ds(pl.multiple_of(i * block, block), block)
        z = nn(w_in_t[...], x[:, cols]) + jnp.concatenate([b_t[...]] * (block // 128), axis=1)
        embed[:, cols] = silu(z).astype(BF16)
        return 0

    lax.fori_loop(0, blocks, embed_block, 0)

    order = (opp_m, right_m, left_m, m)

    def pick_block(base):
        ids = lax.broadcasted_iota(jnp.int32, (quarter, points), 0) + base
        return (ids == rel[...]).astype(F32).astype(BF16)

    for k in range(4):
        rows = pl.ds(pl.multiple_of(nodes + order[k] * quarter, 16), quarter)
        onehot[rows, :] = pick_block(nodes + order[k] * quarter)
        send_n[k] = nt(onehot[rows, :], embed[...]).astype(BF16)
        send("n%d" % k, send_n.at[k], recv_n.at[k], up)
    for k in range(4):
        rows = pl.ds(pl.multiple_of(order[k] * quarter, 16), quarter)
        onehot[rows, :] = pick_block(order[k] * quarter)
        part[k] = nt(onehot[rows, :], embed[...])

    arrived("wr", qkv_part(m, q0, hq))
    arrived("or", wo_part(m, o0, ho))
    send("w2r", qkv_part(left_m, q0, hq // 2), qkv_part(left_m, q0, hq // 2), right)
    send("o2r", wo_part(left_m, o0, ho // 2), wo_part(left_m, o0, ho // 2), right)
    send("ws0", qkv_part(left_m, q0, hq), qkv_part(left_m, q0, hq), sibling)
    send("os0", wo_part(left_m, o0, ho), wo_part(left_m, o0, ho), sibling)
    arrived("wl", qkv_part(m, q0, hq))
    arrived("ol", wo_part(m, o0, ho))
    send("w2l", qkv_part(right_m, q0 + hq // 2, hq // 2), qkv_part(right_m, q0 + hq // 2, hq // 2), left)
    send("o2l", wo_part(right_m, o0 + ho // 2, ho // 2), wo_part(right_m, o0 + ho // 2, ho // 2), left)
    send("ws1", qkv_part(right_m, q0, hq), qkv_part(right_m, q0, hq), sibling)
    send("os1", wo_part(right_m, o0, ho), wo_part(right_m, o0, ho), sibling)

    lo, hi = pl.ds(0, half), pl.ds(half, half)
    arrived("n0", recv_n.at[0])
    ra[...] = (part[0] + recv_n[0].astype(F32)).astype(BF16)
    send("ar", ra.at[lo], ra_l, right)
    send("al", ra.at[hi], ra_r, left)
    arrived("n1", recv_n.at[1])
    rb[0, hi] = (part[1, hi] + recv_n[1, hi].astype(F32)).astype(BF16)
    send("br1", rb.at[0, hi], rb_l.at[hi], right)
    arrived("n2", recv_n.at[2])
    rb[1, lo] = (part[2, lo] + recv_n[2, lo].astype(F32)).astype(BF16)
    send("bl0", rb.at[1, lo], rb_r.at[lo], left)
    arrived("ar", ra_l)
    rb[0, lo] = (part[1, lo] + recv_n[1, lo].astype(F32) + ra_l[...].astype(F32)).astype(BF16)
    send("br0", rb.at[0, lo], rb_l.at[lo], right)
    arrived("al", ra_r)
    rb[1, hi] = (part[2, hi] + recv_n[2, hi].astype(F32) + ra_r[...].astype(F32)).astype(BF16)
    send("bl1", rb.at[1, hi], rb_r.at[hi], left)
    arrived("n3", recv_n.at[3])

    slots_all = jnp.transpose(nbr_ref[...])
    s = slots_all - (here - nodes)
    s = jnp.where(s < 0, s + total, s)
    slots[...] = jnp.where(s >= total, s - total, s)
    span = 3 * nodes

    def count_block(i, _):
        rows = slots[pl.ds(pl.multiple_of(m * quarter + i * 8, 8), 8), :]
        ids = lax.broadcasted_iota(jnp.int32, (8, span), 1)
        count = jnp.zeros((8, span), F32)
        for k in range(neighbours):
            count = count + (rows[:, k:k + 1] == ids).astype(F32)
        bias[pl.ds(pl.multiple_of(i * 8, 8), 8), :] = jnp.where(count > 0.0, jnp.log2(count), ABSENT)
        return 0

    lax.fori_loop(0, quarter // 8, count_block, 0)

    arrived("w2r", qkv_part(opp_m, q0, hq // 2))
    arrived("o2r", wo_part(opp_m, o0, ho // 2))
    send("ws2", qkv_part(opp_m, q0, hq // 2), qkv_part(opp_m, q0, hq // 2), sibling)
    send("os2", wo_part(opp_m, o0, ho // 2), wo_part(opp_m, o0, ho // 2), sibling)
    arrived("w2l", qkv_part(opp_m, q0, hq // 2))
    arrived("o2l", wo_part(opp_m, o0, ho // 2))
    send("ws3", qkv_part(opp_m, q0 + hq // 2, hq // 2), qkv_part(opp_m, q0 + hq // 2, hq // 2), sibling)
    send("os3", wo_part(opp_m, o0 + ho // 2, ho // 2), wo_part(opp_m, o0 + ho // 2, ho // 2), sibling)

    for name, ref in (("br0", rb_l.at[lo]), ("br1", rb_l.at[hi]), ("bl0", rb_r.at[lo]), ("bl1", rb_r.at[hi])):
        arrived(name, ref)
    mesh_in = part[3] + recv_n[3].astype(F32) + rb_l[...].astype(F32) + rb_r[...].astype(F32)
    mean = jnp.mean(mesh_in * mesh_in, axis=-1, keepdims=True)
    state = (mesh_in * lax.rsqrt(mean + 1e-05) * gain_ref[...]).astype(BF16)

    def rows_of(ref, slot, q, start=0, size=quarter):
        return ref.at[pl.ds(pl.multiple_of(slot * nodes + q * quarter + start, 16), size)]

    own = rows_of(st, 1, m)
    own[...] = state

    def gather_ring(ref, slot, tag):
        send(tag + "r", rows_of(ref, slot, m), rows_of(ref, slot, m), right)
        send(tag + "l", rows_of(ref, slot, m), rows_of(ref, slot, m), left)
        yield 0, (m, 0, quarter)
        arrived(tag + "r", rows_of(ref, slot, left_m))
        send(tag + "2r", rows_of(ref, slot, left_m, 0, half), rows_of(ref, slot, left_m, 0, half), right)
        yield 1, (left_m, 0, quarter)
        arrived(tag + "l", rows_of(ref, slot, right_m))
        send(tag + "2l", rows_of(ref, slot, right_m, half, half), rows_of(ref, slot, right_m, half, half), left)
        yield 2, (right_m, 0, quarter)
        arrived(tag + "2r", rows_of(ref, slot, opp_m, 0, half))
        yield 3, (opp_m, 0, half)
        arrived(tag + "2l", rows_of(ref, slot, opp_m, half, half))
        yield 4, (opp_m, half, half)

    for i, (q, start, size) in gather_ring(st, 1, "s"):
        send("su%d" % i, rows_of(st, 1, q, start, size), rows_of(st, 0, q, start, size), up)
        send("sd%d" % i, rows_of(st, 1, q, start, size), rows_of(st, 2, q, start, size), down)

    for i, h in enumerate((left_m, right_m)):
        arrived("ws%d" % i, qkv_part(h, hq - q0, hq))
        arrived("os%d" % i, wo_part(h, ho - o0, ho))
    for i in (2, 3):
        arrived("ws%d" % i, qkv_part(opp_m, hq - q0, hq // 2))
        arrived("os%d" % i, wo_part(opp_m, ho - o0, ho // 2))
    scale = LOG2_E * head_width ** -0.5
    for h in range(heads):
        q = nn(own[...], wqkv[h, 0]).astype(BF16)
        qp[pl.ds(h * quarter, quarter), :] = (nt(q, wqkv[h, 1]) * scale).astype(BF16)

    loads["wdec"].wait()
    wdec_t[...] = jnp.transpose(wdec[...].astype(F32)).astype(BF16)

    def e2_block(i, _):
        cols = pl.ds(pl.multiple_of(i * block, block), block)
        e2[:, cols] = nn(wdec_t[...], embed[:, cols])
        return 0

    lax.fori_loop(0, blocks, e2_block, 0)

    for i in range(5):
        size = quarter if i < 3 else half
        arrived("su%d" % i, rows_of(st, 0, 0, 0, size))
        arrived("sd%d" % i, rows_of(st, 0, 0, 0, size))

    def attend(h, _):
        rows = pl.ds(pl.multiple_of(h * quarter, 16), quarter)
        sc = nt(qp[rows, :], st[...]) + bias[...]
        top = jnp.max(sc, axis=-1, keepdims=True)
        raised = jnp.exp2(sc - top)
        norm = jnp.sum(raised, axis=-1, keepdims=True)
        mixed = nn(raised.astype(BF16), st[...]) / norm
        v = nn(mixed.astype(BF16), wqkv[h, 2]).astype(BF16)
        mix[...] += nn(v, wo[h])
        return 0

    mix[...] = own[...].astype(F32)
    lax.fori_loop(0, heads, attend, 0)
    mesh_out = mix[...].astype(BF16)
    rows_of(md, 0, m)[...] = nn(mesh_out, wdec[...]).astype(BF16)

    for i, (q, start, size) in gather_ring(md, 0, "m"):
        send("md%d" % i, rows_of(md, 0, q, start, size), rows_of(md, 1, q, start, size), down)

    md_t[...] = jnp.transpose(md[pl.ds(0, nodes), :].astype(F32)).astype(BF16)

    def own_block(i, _):
        cols = pl.ds(pl.multiple_of(i * block, block), block)
        e2[:, cols] += nn(md_t[...], onehot[pl.ds(0, nodes), cols])
        return 0

    lax.fori_loop(0, blocks, own_block, 0)

    loads["whead"].wait()
    for i in range(5):
        size = quarter if i < 3 else half
        arrived("md%d" % i, rows_of(md, 1, 0, 0, size))
    md_t[...] = jnp.transpose(md[pl.ds(nodes, nodes), :].astype(F32)).astype(BF16)

    def last_block(i, _):
        cols = pl.ds(pl.multiple_of(i * block, block), block)
        z = e2[:, cols] + nn(md_t[...], onehot[pl.ds(nodes, nodes), cols])
        out_ref[:, cols] = nn(whead[...], silu(z).astype(BF16))
        return 0

    lax.fori_loop(0, blocks, last_block, 0)

    for c in started:
        c.wait_send()


def on_device(grid_state, targets, neighbours, w_in, b_in, mesh_gain, w_qkv, w_out, w_dec, w_head):
    points, channels = grid_state.shape
    nodes, nbr = neighbours.shape
    width = w_in.shape[1]
    quarter = nodes // 4
    half = quarter // 2
    span = 3 * nodes
    heads = 4
    head_width = w_qkv.shape[2]
    out_width = w_head.shape[1]
    regions = lax.axis_size("region")
    vmem = pl.BlockSpec(memory_space=pltpu.VMEM)
    anyw = pl.BlockSpec(memory_space=pl.ANY)
    V = pltpu.VMEM
    out = pl.pallas_call(
        functools.partial(kernel, regions),
        out_shape=jax.ShapeDtypeStruct((out_width, points), F32),
        in_specs=[anyw, vmem, vmem, anyw, vmem, vmem, anyw, anyw, anyw, anyw],
        out_specs=vmem,
        scratch_shapes=[
            V((channels, points), BF16), V((channels, width), BF16), V((width, channels), BF16),
            V((width, 128), F32), V((heads, 3, width, head_width), BF16), V((heads, head_width, width), BF16),
            V((width, width), BF16), V((width, width), BF16), V((out_width, width), BF16),
            V((1, points), jnp.int32), V((nodes, nbr), jnp.int32), V((2 * nodes, points), BF16),
            V((width, points), BF16), V((width, points), F32),
            V((4, quarter, width), BF16), V((4, quarter, width), BF16), V((4, quarter, width), F32),
            V((quarter, width), BF16), V((half, width), BF16), V((half, width), BF16),
            V((2, quarter, width), BF16), V((quarter, width), BF16), V((quarter, width), BF16),
            V((span, width), BF16), V((heads * quarter, width), BF16), V((quarter, span), F32),
            V((quarter, width), F32), V((2 * nodes, width), BF16), V((width, nodes), BF16),
            pltpu.SemaphoreType.DMA((len(NAMES),)), pltpu.SemaphoreType.DMA((len(NAMES),)),
            pltpu.SemaphoreType.DMA((6,)),
        ],
        compiler_params=pltpu.CompilerParams(
            collective_id=0, has_side_effects=True, vmem_limit_bytes=56 * 1024 * 1024
        ),
        cost_estimate=pl.CostEstimate(flops=10 * 10 ** 9, bytes_accessed=4 * 10 ** 6, transcendentals=3 * 10 ** 6),
    )(
        grid_state.T, targets.reshape(1, points), neighbours.T, w_in, b_in.reshape(1, width),
        mesh_gain.reshape(1, width), w_qkv, w_out, w_dec, w_head.T,
    )
    return out.T


def solution(mesh):
    placed = (
        P(("region", "mp"), None),
        P(("region", "mp")),
        P("region", None),
        P(),
        P(),
        P(),
        P(None, None, "mp"),
        P("mp", None),
        P(),
        P(),
    )
    return jax.shard_map(
        on_device, mesh=mesh, in_specs=placed, out_specs=P(("region", "mp"), None), check_vma=False
    )
```

```python
import functools

import jax
import jax.numpy as jnp
from jax import lax
from jax.experimental import pallas as pl
from jax.experimental.pallas import tpu as pltpu
from jax.sharding import PartitionSpec as P

MESH = pl.DeviceIdType.MESH
BF16 = jnp.bfloat16
F32 = jnp.float32
LOG2_E = 1.4426950408889634
ABSENT = -1e30

NAMES = (
    *("wr", "wl", "w2r", "w2l", "ws0", "ws1", "ws2", "ws3"),
    *("vr", "vl", "v2r", "v2l", "vs0", "vs1", "vs2", "vs3"),
    *("or", "ol", "o2r", "o2l", "os0", "os1", "os2", "os3"),
    *("n0", "n1", "n2", "n3"),
    *("ar", "al", "br0", "br1", "bl0", "bl1"),
    *("sr0", "sr1", "sl0", "sl1", "sf0", "sf1"),
    *("su0", "su1", "su2", "su3", "su4", "su5", "su6"),
    *("sd0", "sd1", "sd2", "sd3", "sd4", "sd5", "sd6"),
    *("mr0", "mr1", "ml0", "ml1", "mf0", "mf1"),
    *("md0", "md1", "md2", "md3", "md4", "md5", "md6"),
)
INDEX = {name: i for i, name in enumerate(NAMES)}


def nt(a, b):
    return lax.dot_general(a, b, (((1,), (1,)), ((), ())), preferred_element_type=F32)


def nn(a, b):
    return jnp.dot(a, b, preferred_element_type=F32)


def silu(z):
    half = 0.5 * z
    return half + half * jnp.tanh(half)


def kernel(
    regions,
    x_hbm, targets_ref, nbr_ref, w_in_hbm, b_ref, gain_ref, wqkv_hbm, wo_hbm, wdec_hbm, whead_hbm,
    out_ref,
    x, w_in, w_in_t, b_t, wqkv, wo, wdec, wdec_t, whead,
    rel, slots, own_slots, code_hi, code_lo, onehot, embed, e2,
    send_n, recv_n, part, ra, ra_l, ra_r, rb, rb_l, rb_r,
    st, qp, bias, acc, top, norm, mixed, md, md_t,
    ssem, rsem, lsem,
):
    r = lax.axis_index("region")
    m = lax.axis_index("mp")
    mps = 4
    up = (lax.rem(r + 1, regions), m)
    down = (lax.rem(r + regions - 1, regions), m)
    right_m = lax.rem(m + 1, mps)
    left_m = lax.rem(m + mps - 1, mps)
    opp_m = lax.rem(m + 2, mps)
    right = (r, right_m)
    left = (r, left_m)
    core = lax.rem(r, 2)
    sibling = (r + 1 - 2 * core, m)

    points = x.shape[1]
    width = embed.shape[0]
    quarter = st.shape[0] // 12
    nodes = 4 * quarter
    half = quarter // 2
    span = 3 * nodes
    neighbours = slots.shape[1]
    heads, head_width = wo.shape[0], wo.shape[1]

    started = []

    def send(name, src, dst, dev):
        i = INDEX[name]
        c = pltpu.make_async_remote_copy(
            src_ref=src, dst_ref=dst, send_sem=ssem.at[i], recv_sem=rsem.at[i],
            device_id=dev, device_id_type=MESH,
        )
        c.start()
        started.append(c)

    def arrived(name, dst, shift=0):
        i = INDEX[name] + shift
        pltpu.make_async_remote_copy(
            src_ref=dst, dst_ref=dst, send_sem=ssem.at[i], recv_sem=rsem.at[i],
            device_id=right, device_id_type=MESH,
        ).wait_recv()

    loads = {}
    for i, (name, src, dst) in enumerate((
        ("w_in", w_in_hbm, w_in), ("x", x_hbm, x), ("wqkv", wqkv_hbm, wqkv.at[m]),
        ("wo", wo_hbm, wo.at[m]), ("wdec", wdec_hbm, wdec), ("whead", whead_hbm, whead),
    )):
        loads[name] = pltpu.make_async_copy(src, dst, lsem.at[i])
        loads[name].start()

    barrier = pltpu.get_barrier_semaphore()
    for dev in (up, down, right, left):
        pl.semaphore_signal(barrier, inc=1, device_id=dev, device_id_type=MESH)

    here = r * nodes
    total = regions * nodes
    t = targets_ref[...] - here
    rel[...] = jnp.where(t < 0, t + total, t)
    b_t[...] = jnp.transpose(jnp.broadcast_to(b_ref[...], (128, width)))
    loads["w_in"].wait()
    w_in_t[...] = jnp.transpose(w_in[...].astype(F32)).astype(BF16)

    pl.semaphore_wait(barrier, 4)

    hq = width // 2
    ho = head_width // 2
    q0, o0 = core * hq, core * ho
    q1, o1 = hq - q0, ho - o0

    def w_part(h, start, size, ref=None):
        rows = pl.ds(pl.multiple_of(start, 16), size)
        return (wqkv.at[h] if ref is None else ref).at[pl.ds(0, 2), rows, :]

    def v_part(h, start, size, ref=None):
        rows = pl.ds(pl.multiple_of(start, 16), size)
        return (wqkv.at[h] if ref is None else ref).at[2, rows, :]

    def o_part(h, start, size, ref=None):
        rows = pl.ds(pl.multiple_of(start, 16), size)
        return (wo.at[h] if ref is None else ref).at[rows, :]

    kinds = {"w": (w_part, q0, q1, hq, wqkv_hbm), "v": (v_part, q0, q1, hq, wqkv_hbm), "o": (o_part, o0, o1, ho, wo_hbm)}

    def weights_first(tag):
        view, mine, _, size, hbm = kinds[tag]
        for name, dev in (("r", right), ("l", left)):
            send(tag + name, view(m, mine, size, hbm), view(m, mine, size), dev)

    def weights_second(tag):
        view, mine, _, size, _ = kinds[tag]
        arrived(tag + "r", view(left_m, mine, size))
        send(tag + "2r", view(left_m, mine, size // 2), view(left_m, mine, size // 2), right)
        send(tag + "s0", view(left_m, mine, size), view(left_m, mine, size), sibling)
        arrived(tag + "l", view(right_m, mine, size))
        late = mine + size // 2
        send(tag + "2l", view(right_m, late, size // 2), view(right_m, late, size // 2), left)
        send(tag + "s1", view(right_m, mine, size), view(right_m, mine, size), sibling)

    def weights_third(tag):
        view, mine, _, size, _ = kinds[tag]
        arrived(tag + "2r", view(opp_m, mine, size // 2))
        send(tag + "s2", view(opp_m, mine, size // 2), view(opp_m, mine, size // 2), sibling)
        late = mine + size // 2
        arrived(tag + "2l", view(opp_m, late, size // 2))
        send(tag + "s3", view(opp_m, late, size // 2), view(opp_m, late, size // 2), sibling)

    def weights_end(tag):
        view, _, other, size, _ = kinds[tag]
        arrived(tag + "s0", view(left_m, other, size))
        arrived(tag + "s1", view(right_m, other, size))
        arrived(tag + "s2", view(opp_m, other, size // 2))
        arrived(tag + "s3", view(opp_m, other + size // 2, size // 2))

    weights_first("w")

    loads["x"].wait()
    z = nn(w_in_t[...], x[...]) + jnp.concatenate([b_t[...]] * (points // 128), axis=1)
    embed[...] = silu(z).astype(BF16)

    def pick(base):
        ids = lax.broadcasted_iota(jnp.int32, (nodes, points), 0) + base
        return (ids == rel[...]).astype(F32).astype(BF16)

    def rows_of(ref, q, start=0, size=quarter, slot=0):
        return ref.at[pl.ds(pl.multiple_of(slot * nodes + q * quarter + start, 16), size)]

    onehot[pl.ds(nodes, nodes), :] = pick(nodes)
    send_n[...] = nt(onehot[pl.ds(nodes, nodes), :], embed[...]).astype(BF16)
    order = (opp_m, right_m, left_m, m)
    for k in range(4):
        send("n%d" % k, rows_of(send_n, order[k]), rows_of(recv_n, order[k]), up)
    weights_first("v")
    weights_first("o")
    onehot[pl.ds(0, nodes), :] = pick(0)
    part[...] = nt(onehot[pl.ds(0, nodes), :], embed[...])

    weights_second("w")

    def both(q, start=0, size=quarter):
        return rows_of(part, q, start, size)[...] + rows_of(recv_n, q, start, size)[...].astype(F32)

    lo, hi = pl.ds(0, half), pl.ds(half, half)
    arrived("n0", rows_of(recv_n, opp_m))
    ra[...] = both(opp_m).astype(BF16)
    send("ar", ra.at[lo], ra_l, right)
    send("al", ra.at[hi], ra_r, left)

    s = jnp.transpose(nbr_ref[...]) - (here - nodes)
    s = jnp.where(s < 0, s + total, s)
    slots[...] = jnp.where(s >= total, s - total, s)
    own_slots[...] = slots[pl.ds(pl.multiple_of(m * quarter, 8), quarter), :]
    groups = quarter // 8
    for i in range(8):
        piece = own_slots[pl.ds(i, groups, stride=8), :]
        cols = slice(i * neighbours, (i + 1) * neighbours)
        code_hi[:, cols] = (piece >> 7) + i * 16
        code_lo[:, cols] = piece & 127
    together = 5 if groups % 5 == 0 else 4

    def count_groups(j, _):
        ids = lax.broadcasted_iota(jnp.int32, (128, 8 * neighbours), 0)
        for u in range(together):
            g = j * together + u
            high = (ids == code_hi[pl.ds(g, 1), :]).astype(F32).astype(BF16)
            low = (ids == code_lo[pl.ds(g, 1), :]).astype(F32).astype(BF16)
            count = nt(high, low)
            log = jnp.where(count > 0.0, jnp.log2(count), ABSENT).reshape(8, 16, 128)
            for c in range(span // 128):
                bias[pl.ds(pl.multiple_of(g * 8, 8), 8), c * 128:(c + 1) * 128] = log[:, c, :]
        return 0

    lax.fori_loop(0, groups // together, count_groups, 0)

    arrived("n1", rows_of(recv_n, right_m))
    rb[0, hi] = both(right_m, half, half).astype(BF16)
    send("br1", rb.at[0, hi], rb_l.at[hi], right)
    arrived("ar", ra_l)
    rb[0, lo] = (both(right_m, 0, half) + ra_l[...].astype(F32)).astype(BF16)
    send("br0", rb.at[0, lo], rb_l.at[lo], right)
    weights_third("w")

    loads["wdec"].wait()
    wdec_t[...] = jnp.transpose(wdec[...].astype(F32)).astype(BF16)
    e2[...] = nn(wdec_t[...], embed[...])

    arrived("n2", rows_of(recv_n, left_m))
    rb[1, lo] = both(left_m, 0, half).astype(BF16)
    send("bl0", rb.at[1, lo], rb_r.at[lo], left)
    arrived("al", ra_r)
    rb[1, hi] = (both(left_m, half, half) + ra_r[...].astype(F32)).astype(BF16)
    send("bl1", rb.at[1, hi], rb_r.at[hi], left)
    weights_second("v")
    weights_second("o")
    loads["wqkv"].wait()
    loads["wo"].wait()
    weights_end("w")
    arrived("n3", rows_of(recv_n, m))
    for name, ref in (("br1", rb_l.at[hi]), ("br0", rb_l.at[lo]), ("bl0", rb_r.at[lo]), ("bl1", rb_r.at[hi])):
        arrived(name, ref)
    mesh_in = both(m) + rb_l[...].astype(F32) + rb_r[...].astype(F32)
    mean = jnp.mean(mesh_in * mesh_in, axis=-1, keepdims=True)
    state = (mesh_in * lax.rsqrt(mean + 1e-05) * gain_ref[...]).astype(BF16)

    def share(ref, slot, tag, out):
        def view(q, start=0, size=quarter):
            return rows_of(ref, q, start, size, slot)

        def pass_on(i, q, start=0, size=quarter):
            for name, to_slot, dev in out:
                send(name + str(i), view(q, start, size), rows_of(ref, q, start, size, to_slot), dev)

        send(tag + "r0", view(m, 0, half), view(m, 0, half), right)
        send(tag + "l1", view(m, half, half), view(m, half, half), left)
        pass_on(0, m)
        send(tag + "r1", view(m, half, half), view(m, half, half), right)
        send(tag + "l0", view(m, 0, half), view(m, 0, half), left)
        yield
        arrived(tag + "r0", view(left_m, 0, half))
        send(tag + "f0", view(left_m, 0, half), view(left_m, 0, half), right)
        pass_on(1, left_m, 0, half)
        arrived(tag + "l1", view(right_m, half, half))
        send(tag + "f1", view(right_m, half, half), view(right_m, half, half), left)
        pass_on(2, right_m, half, half)
        yield
        arrived(tag + "r1", view(left_m, half, half))
        pass_on(3, left_m, half, half)
        arrived(tag + "l0", view(right_m, 0, half))
        pass_on(4, right_m, 0, half)
        yield
        arrived(tag + "f0", view(opp_m, 0, half))
        pass_on(5, opp_m, 0, half)
        arrived(tag + "f1", view(opp_m, half, half))
        pass_on(6, opp_m, half, half)
        yield

    def all_passed(ref, name, slot, shift=0):
        for i in range(7):
            arrived(name + str(i), rows_of(ref, 0, 0, half if i else quarter, slot), shift)

    own = rows_of(st, m, slot=1)
    own[...] = state
    steps = share(st, 1, "s", (("su", 0, up), ("sd", 2, down)))
    next(steps)

    scale = LOG2_E * head_width ** -0.5
    queries = [nn(state, wqkv[h, 0]).astype(BF16) for h in range(heads)]
    for h in range(heads):
        qp[pl.ds(h * quarter, quarter), :] = (nt(queries[h], wqkv[h, 1]) * scale).astype(BF16)
    next(steps)
    weights_third("v")
    weights_third("o")
    next(steps)
    next(steps)

    def attend(slot, first):
        rows = pl.ds(pl.multiple_of(slot * nodes, 128), nodes)
        score = nt(qp[...], st[rows, :])
        here_bias = bias[:, rows]
        raised = []
        scales = []
        for h in range(heads):
            masked = score[h * quarter:(h + 1) * quarter] + here_bias
            new = jnp.max(masked, axis=-1, keepdims=True)
            if not first:
                new = jnp.maximum(new, top[h])
                scales.append(jnp.exp2(top[h] - new))
            power = jnp.exp2(masked - new)
            count = jnp.sum(power, axis=-1, keepdims=True)
            norm[h] = count if first else norm[h] * scales[h] + count
            top[h] = new
            raised.append(power.astype(BF16))
        summed = nn(jnp.concatenate(raised, axis=0), st[rows, :])
        for h in range(heads):
            part_h = summed[h * quarter:(h + 1) * quarter]
            acc[h] = part_h if first else acc[h] * scales[h] + part_h

    attend(1, True)
    all_passed(st, "su", 2 - 2 * core, (INDEX["sd0"] - INDEX["su0"]) * (1 - core))
    attend(2 - 2 * core, False)
    weights_end("v")
    weights_end("o")
    all_passed(st, "su", 2 * core, (INDEX["sd0"] - INDEX["su0"]) * core)
    attend(2 * core, False)

    for h in range(heads):
        out_h = nn((acc[h] / norm[h]).astype(BF16), wqkv[h, 2])
        mixed[:, h * head_width:(h + 1) * head_width] = out_h.astype(BF16)
    attended = nn(mixed[...], wo[...].reshape(heads * head_width, width))
    mesh_out = (own[...].astype(F32) + attended).astype(BF16)
    rows_of(md, m)[...] = nn(mesh_out, wdec[...]).astype(BF16)

    for _ in share(md, 0, "m", (("md", 1, down),)):
        pass

    md_t[...] = jnp.transpose(md[pl.ds(0, nodes), :].astype(F32)).astype(BF16)
    e2[...] += nn(md_t[...], onehot[pl.ds(0, nodes), :])
    loads["whead"].wait()
    all_passed(md, "md", 1)
    md_t[...] = jnp.transpose(md[pl.ds(nodes, nodes), :].astype(F32)).astype(BF16)
    z = e2[...] + nn(md_t[...], onehot[pl.ds(nodes, nodes), :])
    out_ref[...] = nn(whead[...], silu(z).astype(BF16))

    for c in started:
        c.wait_send()


def on_device(grid_state, targets, neighbours, w_in, b_in, mesh_gain, w_qkv, w_out, w_dec, w_head):
    points, channels = grid_state.shape
    nodes, nbr = neighbours.shape
    width = w_in.shape[1]
    quarter = nodes // 4
    half = quarter // 2
    span = 3 * nodes
    heads = 4
    head_width = w_qkv.shape[2]
    out_width = w_head.shape[1]
    regions = lax.axis_size("region")
    vmem = pl.BlockSpec(memory_space=pltpu.VMEM)
    anyw = pl.BlockSpec(memory_space=pl.ANY)
    V = pltpu.VMEM
    out = pl.pallas_call(
        functools.partial(kernel, regions),
        out_shape=jax.ShapeDtypeStruct((out_width, points), F32),
        in_specs=[anyw, vmem, vmem, anyw, vmem, vmem, anyw, anyw, anyw, anyw],
        out_specs=vmem,
        scratch_shapes=[
            V((channels, points), BF16), V((channels, width), BF16), V((width, channels), BF16),
            V((width, 128), F32), V((heads, 3, width, head_width), BF16), V((heads, head_width, width), BF16),
            V((width, width), BF16), V((width, width), BF16), V((out_width, width), BF16),
            V((1, points), jnp.int32), V((nodes, nbr), jnp.int32), V((quarter, nbr), jnp.int32),
            V((quarter // 8, 8 * nbr), jnp.int32), V((quarter // 8, 8 * nbr), jnp.int32),
            V((2 * nodes, points), BF16), V((width, points), BF16), V((width, points), F32),
            V((nodes, width), BF16), V((nodes, width), BF16), V((nodes, width), F32),
            V((quarter, width), BF16), V((half, width), BF16), V((half, width), BF16),
            V((2, quarter, width), BF16), V((quarter, width), BF16), V((quarter, width), BF16),
            V((span, width), BF16), V((heads * quarter, width), BF16), V((quarter, span), F32),
            V((heads, quarter, width), F32), V((heads, quarter, 1), F32), V((heads, quarter, 1), F32),
            V((quarter, heads * head_width), BF16), V((2 * nodes, width), BF16), V((width, nodes), BF16),
            pltpu.SemaphoreType.DMA((len(NAMES),)), pltpu.SemaphoreType.DMA((len(NAMES),)),
            pltpu.SemaphoreType.DMA((6,)),
        ],
        compiler_params=pltpu.CompilerParams(
            collective_id=0, has_side_effects=True, vmem_limit_bytes=56 * 1024 * 1024
        ),
        cost_estimate=pl.CostEstimate(flops=10 * 10 ** 9, bytes_accessed=4 * 10 ** 6, transcendentals=3 * 10 ** 6),
    )(
        grid_state.T, targets.reshape(1, points), neighbours.T, w_in, b_in.reshape(1, width),
        mesh_gain.reshape(1, width), w_qkv, w_out, w_dec, w_head.T,
    )
    return out.T


def solution(mesh):
    placed = (
        P(("region", "mp"), None),
        P(("region", "mp")),
        P("region", None),
        P(),
        P(),
        P(),
        P(None, None, "mp"),
        P("mp", None),
        P(),
        P(),
    )
    return jax.shard_map(
        on_device, mesh=mesh, in_specs=placed, out_specs=P(("region", "mp"), None), check_vma=False
    )
```

```python
import functools

import jax
import jax.numpy as jnp
from jax import lax
from jax.experimental import pallas as pl
from jax.experimental.pallas import tpu as pltpu
from jax.sharding import PartitionSpec as P

MESH = pl.DeviceIdType.MESH
BF16 = jnp.bfloat16
F32 = jnp.float32
LOG2_E = 1.4426950408889634
ABSENT = -1e30

NAMES = (
    *("wr", "wl", "w2r", "w2l", "ws0", "ws1", "ws2", "ws3"),
    *("vr", "vl", "v2r", "v2l", "vs0", "vs1", "vs2", "vs3"),
    *("or", "ol", "o2r", "o2l", "os0", "os1", "os2", "os3"),
    *("n0", "n1", "n2", "n3"),
    *("ar", "al", "br0", "br1", "bl0", "bl1"),
    *("sr0", "sr1", "sl0", "sl1", "sf0", "sf1"),
    *("su0", "su1", "su2", "su3", "su4", "su5", "su6"),
    *("sd0", "sd1", "sd2", "sd3", "sd4", "sd5", "sd6"),
    *("mr0", "mr1", "ml0", "ml1", "mf0", "mf1"),
    *("md0", "md1", "md2", "md3", "md4", "md5", "md6"),
)
INDEX = {name: i for i, name in enumerate(NAMES)}


def nt(a, b):
    return lax.dot_general(a, b, (((1,), (1,)), ((), ())), preferred_element_type=F32)


def nn(a, b):
    return jnp.dot(a, b, preferred_element_type=F32)


def silu(z):
    half = 0.5 * z
    return half + half * jnp.tanh(half)


def kernel(
    regions,
    x_hbm, targets_ref, nbr_hbm, w_in_hbm, b_ref, gain_ref, wqkv_hbm, wo_hbm, wdec_hbm, whead_hbm,
    out_ref,
    x, nbr, w_in, w_in_t, b_t, wqkv, wo, wdec, wdec_t, whead,
    rel, slots, own_slots, code_hi, code_lo, onehot, embed, e2,
    send_n, recv_n, part, ra, ra_l, ra_r, rb, rb_l, rb_r,
    st, qp, bias, acc, top, norm, mixed, md, md_t,
    ssem, rsem, lsem,
):
    r = lax.axis_index("region")
    m = lax.axis_index("mp")
    mps = 4
    up = (lax.rem(r + 1, regions), m)
    down = (lax.rem(r + regions - 1, regions), m)
    right_m = lax.rem(m + 1, mps)
    left_m = lax.rem(m + mps - 1, mps)
    opp_m = lax.rem(m + 2, mps)
    right = (r, right_m)
    left = (r, left_m)
    core = lax.rem(r, 2)
    sibling = (r + 1 - 2 * core, m)

    points = x.shape[1]
    width = embed.shape[0]
    quarter = st.shape[0] // 12
    nodes = 4 * quarter
    half = quarter // 2
    span = 3 * nodes
    neighbours = slots.shape[1]
    heads, head_width = wo.shape[0], wo.shape[1]

    started = []

    def send(name, src, dst, dev):
        i = INDEX[name]
        c = pltpu.make_async_remote_copy(
            src_ref=src, dst_ref=dst, send_sem=ssem.at[i], recv_sem=rsem.at[i],
            device_id=dev, device_id_type=MESH,
        )
        c.start()
        started.append(c)

    def arrived(name, dst, shift=0):
        i = INDEX[name] + shift
        pltpu.make_async_remote_copy(
            src_ref=dst, dst_ref=dst, send_sem=ssem.at[i], recv_sem=rsem.at[i],
            device_id=right, device_id_type=MESH,
        ).wait_recv()

    loads = {}
    for i, (name, src, dst) in enumerate((
        ("w_in", w_in_hbm, w_in), ("x", x_hbm, x), ("wqkv", wqkv_hbm, wqkv.at[m]),
        ("wo", wo_hbm, wo.at[m]), ("wdec", wdec_hbm, wdec), ("whead", whead_hbm, whead), ("nbr", nbr_hbm, nbr),
    )):
        loads[name] = pltpu.make_async_copy(src, dst, lsem.at[i])
        loads[name].start()

    barrier = pltpu.get_barrier_semaphore()
    for dev in (up, down, right, left):
        pl.semaphore_signal(barrier, inc=1, device_id=dev, device_id_type=MESH)

    here = r * nodes
    total = regions * nodes
    t = targets_ref[...] - here
    rel[...] = jnp.where(t < 0, t + total, t)
    b_t[...] = jnp.transpose(jnp.broadcast_to(b_ref[...], (128, width)))
    pl.semaphore_wait(barrier, 4)

    hq = width // 2
    ho = head_width // 2
    q0, o0 = core * hq, core * ho
    q1, o1 = hq - q0, ho - o0

    def w_part(h, start, size, ref=None):
        rows = pl.ds(pl.multiple_of(start, 16), size)
        return (wqkv.at[h] if ref is None else ref).at[pl.ds(0, 2), rows, :]

    def v_part(h, start, size, ref=None):
        rows = pl.ds(pl.multiple_of(start, 16), size)
        return (wqkv.at[h] if ref is None else ref).at[2, rows, :]

    def o_part(h, start, size, ref=None):
        rows = pl.ds(pl.multiple_of(start, 16), size)
        return (wo.at[h] if ref is None else ref).at[rows, :]

    kinds = {"w": (w_part, q0, q1, hq, wqkv_hbm), "v": (v_part, q0, q1, hq, wqkv_hbm), "o": (o_part, o0, o1, ho, wo_hbm)}

    def weights_first(tag):
        view, mine, _, size, hbm = kinds[tag]
        for name, dev in (("r", right), ("l", left)):
            send(tag + name, view(m, mine, size, hbm), view(m, mine, size), dev)

    def weights_second(tag):
        view, mine, _, size, _ = kinds[tag]
        arrived(tag + "r", view(left_m, mine, size))
        send(tag + "2r", view(left_m, mine, size // 2), view(left_m, mine, size // 2), right)
        send(tag + "s0", view(left_m, mine, size), view(left_m, mine, size), sibling)
        arrived(tag + "l", view(right_m, mine, size))
        late = mine + size // 2
        send(tag + "2l", view(right_m, late, size // 2), view(right_m, late, size // 2), left)
        send(tag + "s1", view(right_m, mine, size), view(right_m, mine, size), sibling)

    def weights_third(tag):
        view, mine, _, size, _ = kinds[tag]
        arrived(tag + "2r", view(opp_m, mine, size // 2))
        send(tag + "s2", view(opp_m, mine, size // 2), view(opp_m, mine, size // 2), sibling)
        late = mine + size // 2
        arrived(tag + "2l", view(opp_m, late, size // 2))
        send(tag + "s3", view(opp_m, late, size // 2), view(opp_m, late, size // 2), sibling)

    def weights_end(tag):
        view, _, other, size, _ = kinds[tag]
        arrived(tag + "s0", view(left_m, other, size))
        arrived(tag + "s1", view(right_m, other, size))
        arrived(tag + "s2", view(opp_m, other, size // 2))
        arrived(tag + "s3", view(opp_m, other + size // 2, size // 2))

    for tag in ("w", "v", "o"):
        weights_first(tag)

    loads["w_in"].wait()
    w_in_t[...] = jnp.transpose(w_in[...].astype(F32)).astype(BF16)
    loads["x"].wait()
    z = nn(w_in_t[...], x[...]) + jnp.concatenate([b_t[...]] * (points // 128), axis=1)
    embed[...] = silu(z).astype(BF16)

    order = (opp_m, right_m, left_m, m)

    def rows_of(ref, q, start=0, size=quarter, slot=0):
        first = slot * nodes + q * quarter + start
        return ref.at[pl.ds(first if isinstance(first, int) else pl.multiple_of(first, 16), size)]

    def sums(slot, k, count):
        for i in range(k, k + count):
            ids = lax.broadcasted_iota(jnp.int32, (quarter, points), 0) + (slot * nodes + order[i] * quarter)
            rows_of(onehot, i, slot=slot)[...] = (ids == rel[...]).astype(F32).astype(BF16)
        return nt(rows_of(onehot, k, 0, count * quarter, slot)[...], embed[...])

    for k in (0, 2):
        rows_of(send_n, k, 0, 2 * quarter)[...] = sums(1, k, 2).astype(BF16)
        for i in (k, k + 1):
            send("n%d" % i, rows_of(send_n, i), rows_of(recv_n, i), up)
    part[...] = sums(0, 0, 4)

    for tag in ("w", "v", "o"):
        weights_second(tag)

    def both(q, start=0, size=quarter):
        return rows_of(part, q, start, size)[...] + rows_of(recv_n, q, start, size)[...].astype(F32)

    lo, hi = pl.ds(0, half), pl.ds(half, half)
    arrived("n0", rows_of(recv_n, 0))
    ra[...] = both(0).astype(BF16)
    send("ar", ra.at[lo], ra_l, right)
    send("al", ra.at[hi], ra_r, left)

    loads["nbr"].wait()
    s = jnp.transpose(nbr[...]) - (here - nodes)
    s = jnp.where(s < 0, s + total, s)
    slots[...] = jnp.where(s >= total, s - total, s)
    own_slots[...] = slots[pl.ds(pl.multiple_of(m * quarter, 8), quarter), :]
    groups = quarter // 8
    for i in range(8):
        piece = own_slots[pl.ds(i, groups, stride=8), :]
        cols = slice(i * neighbours, (i + 1) * neighbours)
        code_hi[:, cols] = (piece >> 7) + i * 16
        code_lo[:, cols] = piece & 127
    together = 5 if groups % 5 == 0 else 4

    def count_groups(j, _):
        ids = lax.broadcasted_iota(jnp.int32, (128, 8 * neighbours), 0)
        for u in range(together):
            g = j * together + u
            high = (ids == code_hi[pl.ds(g, 1), :]).astype(F32).astype(BF16)
            low = (ids == code_lo[pl.ds(g, 1), :]).astype(F32).astype(BF16)
            count = nt(high, low)
            log = jnp.where(count > 0.0, jnp.log2(count), ABSENT).reshape(8, 16, 128)
            for c in range(span // 128):
                bias[pl.ds(pl.multiple_of(g * 8, 8), 8), c * 128:(c + 1) * 128] = log[:, c, :]
        return 0

    lax.fori_loop(0, groups // together, count_groups, 0)

    arrived("n1", rows_of(recv_n, 1))
    rb[0, hi] = both(1, half, half).astype(BF16)
    send("br1", rb.at[0, hi], rb_l.at[hi], right)
    arrived("ar", ra_l)
    rb[0, lo] = (both(1, 0, half) + ra_l[...].astype(F32)).astype(BF16)
    send("br0", rb.at[0, lo], rb_l.at[lo], right)
    weights_third("w")

    loads["wdec"].wait()
    wdec_t[...] = jnp.transpose(wdec[...].astype(F32)).astype(BF16)
    e2[...] = nn(wdec_t[...], embed[...])

    arrived("n2", rows_of(recv_n, 2))
    rb[1, lo] = both(2, 0, half).astype(BF16)
    send("bl0", rb.at[1, lo], rb_r.at[lo], left)
    arrived("al", ra_r)
    rb[1, hi] = (both(2, half, half) + ra_r[...].astype(F32)).astype(BF16)
    send("bl1", rb.at[1, hi], rb_r.at[hi], left)
    loads["wqkv"].wait()
    loads["wo"].wait()
    weights_end("w")
    arrived("n3", rows_of(recv_n, 3))
    for name, ref in (("br1", rb_l.at[hi]), ("br0", rb_l.at[lo]), ("bl0", rb_r.at[lo]), ("bl1", rb_r.at[hi])):
        arrived(name, ref)
    mesh_in = both(3) + rb_l[...].astype(F32) + rb_r[...].astype(F32)
    mean = jnp.mean(mesh_in * mesh_in, axis=-1, keepdims=True)
    state = (mesh_in * lax.rsqrt(mean + 1e-05) * gain_ref[...]).astype(BF16)

    def share(ref, slot, tag, out, here_at, there_at):
        def view(at, who, start=0, size=quarter, to_slot=slot):
            return rows_of(ref, at[who], start, size, to_slot)

        def give(name, who, whose, start, dev):
            send(tag + name, view(here_at, who, start, half), view(there_at(who, whose), whose, start, half), dev)

        def got(name, who, start):
            arrived(tag + name, view(here_at, who, start, half))

        def pass_on(i, who, start=0, size=quarter):
            for name, to_slot, dev in out:
                send(name + str(i), view(here_at, who, start, size), view(here_at, who, start, size, to_slot), dev)

        give("r0", "own", "left", 0, right)
        give("l1", "own", "right", half, left)
        pass_on(0, "own")
        give("r1", "own", "left", half, right)
        give("l0", "own", "right", 0, left)
        yield
        got("r0", "left", 0)
        give("f0", "left", "opp", 0, right)
        pass_on(1, "left", 0, half)
        got("l1", "right", half)
        give("f1", "right", "opp", half, left)
        pass_on(2, "right", half, half)
        yield
        got("r1", "left", half)
        pass_on(3, "left", half, half)
        got("l0", "right", 0)
        pass_on(4, "right", 0, half)
        yield
        got("f0", "opp", 0)
        pass_on(5, "opp", 0, half)
        got("f1", "opp", half)
        pass_on(6, "opp", half, half)
        yield

    def all_passed(ref, name, slot, shift=0, which=range(7)):
        for i in which:
            arrived(name + str(i), rows_of(ref, 0, 0, half if i else quarter, slot), shift)

    own = rows_of(st, m, slot=1)
    own[...] = state
    by_number = {"own": m, "left": left_m, "right": right_m, "opp": opp_m}
    steps = share(st, 1, "s", (("su", 0, up), ("sd", 2, down)), by_number, lambda who, whose: {whose: by_number[who]})
    next(steps)

    scale = LOG2_E * head_width ** -0.5
    queries = [nn(state, wqkv[h, 0]).astype(BF16) for h in range(heads)]
    for h in range(heads):
        qp[pl.ds(h * quarter, quarter), :] = (nt(queries[h], wqkv[h, 1]) * scale).astype(BF16)
    next(steps)
    weights_third("v")
    weights_third("o")
    next(steps)
    next(steps)

    def attend(slot, first):
        rows = pl.ds(pl.multiple_of(slot * nodes, 128), nodes)
        score = nt(qp[...], st[rows, :])
        here_bias = bias[:, rows]
        raised = []
        scales = []
        for h in range(heads):
            masked = score[h * quarter:(h + 1) * quarter] + here_bias
            new = jnp.max(masked, axis=-1, keepdims=True)
            if not first:
                new = jnp.maximum(new, top[h])
                scales.append(jnp.exp2(top[h] - new))
            power = jnp.exp2(masked - new)
            count = jnp.sum(power, axis=-1, keepdims=True)
            norm[h] = count if first else norm[h] * scales[h] + count
            top[h] = new
            raised.append(power.astype(BF16))
        summed = nn(jnp.concatenate(raised, axis=0), st[rows, :])
        for h in range(heads):
            part_h = summed[h * quarter:(h + 1) * quarter]
            acc[h] = part_h if first else acc[h] * scales[h] + part_h

    attend(1, True)
    all_passed(st, "su", 2 - 2 * core, (INDEX["sd0"] - INDEX["su0"]) * (1 - core))
    attend(2 - 2 * core, False)
    weights_end("v")
    weights_end("o")
    all_passed(st, "su", 2 * core, (INDEX["sd0"] - INDEX["su0"]) * core)
    attend(2 * core, False)

    for h in range(heads):
        out_h = nn((acc[h] / norm[h]).astype(BF16), wqkv[h, 2])
        mixed[:, h * head_width:(h + 1) * head_width] = out_h.astype(BF16)
    attended = nn(mixed[...], wo[...].reshape(heads * head_width, width))
    mesh_out = (own[...].astype(F32) + attended).astype(BF16)
    rows_of(md, 3)[...] = nn(mesh_out, wdec[...]).astype(BF16)

    by_place = {"own": 3, "left": 2, "right": 1, "opp": 0}
    for _ in share(md, 0, "m", (("md", 1, down),), by_place, lambda who, whose: by_place):
        pass

    def turned(first, count):
        return jnp.transpose(md[pl.ds(first, count), :].astype(F32)).astype(BF16)

    e2[...] += nn(turned(0, nodes), onehot[pl.ds(0, nodes), :])
    loads["whead"].wait()
    all_passed(md, "md", 1, which=range(5))
    late = -(-quarter // 128) * 128
    if late < nodes:
        e2[...] += nn(turned(nodes + late, nodes - late), onehot[pl.ds(nodes + late, nodes - late), :])
    all_passed(md, "md", 1, which=(5, 6))
    md_t[...] = turned(nodes, late)
    block = min(1024, points)
    for i in range(points // block):
        cols = slice(i * block, (i + 1) * block)
        z = e2[:, cols] + nn(md_t[...], onehot[nodes:nodes + late, cols])
        out_ref[:, cols] = nn(whead[...], silu(z).astype(BF16))

    for c in started:
        c.wait_send()


def on_device(grid_state, targets, neighbours, w_in, b_in, mesh_gain, w_qkv, w_out, w_dec, w_head):
    points, channels = grid_state.shape
    nodes, nbr = neighbours.shape
    width = w_in.shape[1]
    quarter = nodes // 4
    half = quarter // 2
    span = 3 * nodes
    heads = 4
    head_width = w_qkv.shape[2]
    out_width = w_head.shape[1]
    regions = lax.axis_size("region")
    vmem = pl.BlockSpec(memory_space=pltpu.VMEM)
    anyw = pl.BlockSpec(memory_space=pl.ANY)
    V = pltpu.VMEM
    out = pl.pallas_call(
        functools.partial(kernel, regions),
        out_shape=pltpu.VMEM((out_width, points), F32),
        in_specs=[anyw, vmem, anyw, anyw, vmem, vmem, anyw, anyw, anyw, anyw],
        out_specs=vmem,
        scratch_shapes=[
            V((channels, points), BF16), V((nbr, nodes), jnp.int32), V((channels, width), BF16), V((width, channels), BF16),
            V((width, 128), F32), V((heads, 3, width, head_width), BF16), V((heads, head_width, width), BF16),
            V((width, width), BF16), V((width, width), BF16), V((out_width, width), BF16),
            V((1, points), jnp.int32), V((nodes, nbr), jnp.int32), V((quarter, nbr), jnp.int32),
            V((quarter // 8, 8 * nbr), jnp.int32), V((quarter // 8, 8 * nbr), jnp.int32),
            V((2 * nodes, points), BF16), V((width, points), BF16), V((width, points), F32),
            V((nodes, width), BF16), V((nodes, width), BF16), V((nodes, width), F32),
            V((quarter, width), BF16), V((half, width), BF16), V((half, width), BF16),
            V((2, quarter, width), BF16), V((quarter, width), BF16), V((quarter, width), BF16),
            V((span, width), BF16), V((heads * quarter, width), BF16), V((quarter, span), F32),
            V((heads, quarter, width), F32), V((heads, quarter, 1), F32), V((heads, quarter, 1), F32),
            V((quarter, heads * head_width), BF16), V((2 * nodes, width), BF16), V((width, -(-quarter // 128) * 128), BF16),
            pltpu.SemaphoreType.DMA((len(NAMES),)), pltpu.SemaphoreType.DMA((len(NAMES),)),
            pltpu.SemaphoreType.DMA((7,)),
        ],
        compiler_params=pltpu.CompilerParams(
            collective_id=0, has_side_effects=True, vmem_limit_bytes=56 * 1024 * 1024
        ),
        cost_estimate=pl.CostEstimate(flops=10 * 10 ** 9, bytes_accessed=4 * 10 ** 6, transcendentals=3 * 10 ** 6),
    )(
        grid_state.T, targets.reshape(1, points), neighbours.T, w_in, b_in.reshape(1, width),
        mesh_gain.reshape(1, width), w_qkv, w_out, w_dec, w_head.T,
    )
    return out.T


def solution(mesh):
    placed = (
        P(("region", "mp"), None),
        P(("region", "mp")),
        P("region", None),
        P(),
        P(),
        P(),
        P(None, None, "mp"),
        P("mp", None),
        P(),
        P(),
    )
    return jax.shard_map(
        on_device, mesh=mesh, in_specs=placed, out_specs=P(("region", "mp"), None), check_vma=False
    )
```

```python
import functools

import jax
import jax.numpy as jnp
from jax import lax
from jax.experimental import pallas as pl
from jax.experimental.pallas import tpu as pltpu
from jax.sharding import PartitionSpec as P

MESH = pl.DeviceIdType.MESH
BF16 = jnp.bfloat16
F32 = jnp.float32
LOG2_E = 1.4426950408889634
ABSENT = -1e30

NAMES = (
    *("or", "ol", "oo", "os0", "os1", "os2"),
    *("n0", "n1", "n2", "n3"),
    *("ar", "al", "br0", "br1", "bl0", "bl1"),
    *("sr0", "sr1", "sl0", "sl1", "sf0", "sf1"),
    *("su0", "su1", "su2", "su3", "su4", "su5", "su6"),
    *("sd0", "sd1", "sd2", "sd3", "sd4", "sd5", "sd6"),
    *("xr", "xl", "xo"),
    *("mr0", "mr1", "ml0", "ml1", "mf0", "mf1"),
    *("md0", "md1", "md2", "md3", "md4", "md5", "md6"),
)
INDEX = {name: i for i, name in enumerate(NAMES)}


def nt(a, b):
    return lax.dot_general(a, b, (((1,), (1,)), ((), ())), preferred_element_type=F32)


def nn(a, b):
    return jnp.dot(a, b, preferred_element_type=F32)


def silu(z):
    half = 0.5 * z
    return half + half * jnp.tanh(half)


def kernel(
    regions,
    x_hbm, targets_ref, nbr_hbm, w_in_hbm, b_ref, gain_ref, wqkv_hbm, wo_hbm, wdec_hbm, whead_hbm,
    out_ref,
    x, nbr, w_in, w_in_t, b_t, wqkv, wo, wdec, wdec_t, whead,
    rel, slots, code_hi, code_lo, onehot, embed, e2,
    send_n, recv_n, part, ra, ra_l, ra_r, rb, rb_l, rb_r,
    st, query, kv, bias, acc, top, norm, mixed, mix_out, md, md_t,
    ssem, rsem, lsem,
):
    r = lax.axis_index("region")
    m = lax.axis_index("mp")
    mps = 4
    up = (lax.rem(r + 1, regions), m)
    down = (lax.rem(r + regions - 1, regions), m)
    right_m = lax.rem(m + 1, mps)
    left_m = lax.rem(m + mps - 1, mps)
    opp_m = lax.rem(m + 2, mps)
    opposite = (r, opp_m)
    right = (r, right_m)
    left = (r, left_m)
    core = lax.rem(r, 2)
    sibling = (r + 1 - 2 * core, m)

    points = x.shape[1]
    width = embed.shape[0]
    nodes = st.shape[0]
    quarter = nodes // 4
    half = quarter // 2
    span = 3 * nodes
    neighbours = slots.shape[1]
    heads, head_width = wo.shape[0], wo.shape[1]

    started = []

    def send(name, src, dst, dev):
        i = INDEX[name]
        c = pltpu.make_async_remote_copy(
            src_ref=src, dst_ref=dst, send_sem=ssem.at[i], recv_sem=rsem.at[i],
            device_id=dev, device_id_type=MESH,
        )
        c.start()
        started.append(c)

    def arrived(name, dst, shift=0):
        i = INDEX[name] + shift
        pltpu.make_async_remote_copy(
            src_ref=dst, dst_ref=dst, send_sem=ssem.at[i], recv_sem=rsem.at[i],
            device_id=right, device_id_type=MESH,
        ).wait_recv()

    loads = {}
    for i, (name, src, dst) in enumerate((
        ("w_in", w_in_hbm, w_in), ("x", x_hbm, x), ("wo", wo_hbm, wo.at[m]), ("wdec", wdec_hbm, wdec), ("whead", whead_hbm, whead), ("nbr", nbr_hbm, nbr),
        *(("w%d" % j, wqkv_hbm.at[j], wqkv.at[:, pl.ds(j * head_width, head_width)]) for j in range(3)),
    )):
        loads[name] = pltpu.make_async_copy(src, dst, lsem.at[i])
        loads[name].start()

    barrier = pltpu.get_barrier_semaphore()
    for dev in (up, down, right, left, opposite):
        pl.semaphore_signal(barrier, inc=1, device_id=dev, device_id_type=MESH)

    here = r * nodes
    total = regions * nodes
    t = targets_ref[...] - here
    rel[...] = jnp.where(t < 0, t + total, t)
    b_t[...] = jnp.transpose(jnp.broadcast_to(b_ref[...], (128, width)))
    pl.semaphore_wait(barrier, 5)

    ho = head_width // 2

    def wo_half(h, which):
        return wo.at[h, pl.ds(pl.multiple_of(which * ho, 16), ho), :]

    for name, dev in (("or", right), ("ol", left), ("oo", opposite)):
        send(name, wo_hbm.at[pl.ds(pl.multiple_of(core * ho, 16), ho), :], wo_half(m, core), dev)

    loads["w_in"].wait()
    w_in_t[...] = jnp.transpose(w_in[...].astype(F32)).astype(BF16)
    loads["x"].wait()
    z = nn(w_in_t[...], x[...]) + jnp.concatenate([b_t[...]] * (points // 128), axis=1)
    embed[...] = silu(z).astype(BF16)

    order = (opp_m, right_m, left_m, m)

    def rows_of(ref, q, start=0, size=quarter, slot=0):
        first = slot * nodes + q * quarter + start
        return ref.at[pl.ds(first if isinstance(first, int) else pl.multiple_of(first, 16), size)]

    def sums(slot, k, count):
        for i in range(k, k + count):
            ids = lax.broadcasted_iota(jnp.int32, (quarter, points), 0) + (slot * nodes + order[i] * quarter)
            rows_of(onehot, i, slot=slot)[...] = (ids == rel[...]).astype(F32).astype(BF16)
        return nt(rows_of(onehot, k, 0, count * quarter, slot)[...], embed[...])

    for k in (0, 2):
        rows_of(send_n, k, 0, 2 * quarter)[...] = sums(1, k, 2).astype(BF16)
        for i in (k, k + 1):
            send("n%d" % i, rows_of(send_n, i), rows_of(recv_n, i), up)
    part[...] = sums(0, 0, 4)

    for i, (name, h) in enumerate((("or", left_m), ("ol", right_m), ("oo", opp_m))):
        arrived(name, wo_half(h, core))
        send("os%d" % i, wo_half(h, core), wo_half(h, core), sibling)

    def both(q, start=0, size=quarter):
        return rows_of(part, q, start, size)[...] + rows_of(recv_n, q, start, size)[...].astype(F32)

    lo, hi = pl.ds(0, half), pl.ds(half, half)
    arrived("n0", rows_of(recv_n, 0))
    ra[...] = both(0).astype(BF16)
    send("ar", ra.at[lo], ra_l, right)
    send("al", ra.at[hi], ra_r, left)

    loads["nbr"].wait()
    s = jnp.transpose(nbr[...]) - (here - nodes)
    s = jnp.where(s < 0, s + total, s)
    slots[...] = jnp.where(s >= total, s - total, s)
    groups = nodes // 8
    for i in range(8):
        piece = slots[pl.ds(i, groups, stride=8), :]
        cols = slice(i * neighbours, (i + 1) * neighbours)
        code_hi[:, cols] = (piece >> 7) + i * 16
        code_lo[:, cols] = piece & 127
    together = 5 if groups % 20 == 0 else 4
    share_of_counts = groups // (4 * together)

    def count_groups(j, _):
        ids = lax.broadcasted_iota(jnp.int32, (128, 8 * neighbours), 0)
        for u in range(together):
            g = j * together + u
            high = (ids == code_hi[pl.ds(g, 1), :]).astype(F32).astype(BF16)
            low = (ids == code_lo[pl.ds(g, 1), :]).astype(F32).astype(BF16)
            count = nt(high, low)
            log = jnp.where(count > 0.0, jnp.log2(count), ABSENT).reshape(8, 16, 128)
            for c in range(span // 128):
                bias[pl.ds(pl.multiple_of(g * 8, 8), 8), c * 128:(c + 1) * 128] = log[:, c, :]
        return 0

    def counts(i):
        lax.fori_loop(i * share_of_counts, (i + 1) * share_of_counts, count_groups, 0)

    counts(0)
    counts(1)

    arrived("n1", rows_of(recv_n, 1))
    rb[0, hi] = both(1, half, half).astype(BF16)
    send("br1", rb.at[0, hi], rb_l.at[hi], right)
    arrived("ar", ra_l)
    rb[0, lo] = (both(1, 0, half) + ra_l[...].astype(F32)).astype(BF16)
    send("br0", rb.at[0, lo], rb_l.at[lo], right)
    arrived("n2", rows_of(recv_n, 2))
    rb[1, lo] = both(2, 0, half).astype(BF16)
    send("bl0", rb.at[1, lo], rb_r.at[lo], left)
    arrived("al", ra_r)
    rb[1, hi] = (both(2, half, half) + ra_r[...].astype(F32)).astype(BF16)
    send("bl1", rb.at[1, hi], rb_r.at[hi], left)
    arrived("n3", rows_of(recv_n, 3))
    for name, ref in (("br1", rb_l.at[hi]), ("br0", rb_l.at[lo]), ("bl0", rb_r.at[lo]), ("bl1", rb_r.at[hi])):
        arrived(name, ref)
    mesh_in = both(3) + rb_l[...].astype(F32) + rb_r[...].astype(F32)
    mean = jnp.mean(mesh_in * mesh_in, axis=-1, keepdims=True)
    state = (mesh_in * lax.rsqrt(mean + 1e-05) * gain_ref[...]).astype(BF16)

    def share(ref, tag, here_at, there_at, pass_on):
        def view(at, who, start=0, size=quarter):
            return rows_of(ref, at[who], start, size)

        def give(name, who, whose, start, dev):
            send(tag + name, view(here_at, who, start, half), view(there_at(who, whose), whose, start, half), dev)

        def got(name, who, start):
            arrived(tag + name, view(here_at, who, start, half))

        give("r0", "own", "left", 0, right)
        give("l1", "own", "right", half, left)
        pass_on(0, "own", 0, quarter)
        give("r1", "own", "left", half, right)
        give("l0", "own", "right", 0, left)
        yield
        got("r0", "left", 0)
        give("f0", "left", "opp", 0, right)
        pass_on(1, "left", 0, half)
        got("l1", "right", half)
        give("f1", "right", "opp", half, left)
        pass_on(2, "right", half, half)
        yield
        got("r1", "left", half)
        pass_on(3, "left", half, half)
        got("l0", "right", 0)
        pass_on(4, "right", 0, half)
        yield
        got("f0", "opp", 0)
        pass_on(5, "opp", 0, half)
        got("f1", "opp", half)
        pass_on(6, "opp", half, half)
        yield

    def all_passed(ref, name, slot, shift=0, which=range(7)):
        for i in which:
            arrived(name + str(i), rows_of(ref, 0, 0, half if i else quarter, slot), shift)

    own = rows_of(st, m)
    own[...] = state
    by_number = {"own": m, "left": left_m, "right": right_m, "opp": opp_m}
    pieces = []
    steps = share(st, "s", by_number, lambda who, whose: {whose: by_number[who]}, lambda *piece: pieces.append(piece))

    def project():
        new = jnp.concatenate([rows_of(st, by_number[who], start, size)[...] for _, who, start, size in pieces], axis=0)
        qkv = nn(new, wqkv[...])
        first = 0
        for i, who, start, size in pieces:
            rows = qkv[first:first + size]
            first += size
            rows_of(query, by_number[who], start, size)[...] = (rows[:, :head_width] * scale).astype(BF16)
            rows_of(kv, by_number[who], start, size, 1)[...] = rows[:, head_width:].astype(BF16)
            for name, slot, dev in (("su", 0, up), ("sd", 2, down)):
                send(name + str(i), rows_of(kv, by_number[who], start, size, 1), rows_of(kv, by_number[who], start, size, slot), dev)
        pieces.clear()

    scale = LOG2_E * head_width ** -0.5
    next(steps)
    for j in range(3):
        loads["w%d" % j].wait()
    project()
    counts(2)
    next(steps)
    project()
    counts(3)
    next(steps)
    project()

    loads["wdec"].wait()
    wdec_t[...] = jnp.transpose(wdec[...].astype(F32)).astype(BF16)
    e2[...] = nn(wdec_t[...], embed[...])
    next(steps)
    project()

    def attend(slot, first):
        rows = pl.ds(pl.multiple_of(slot * nodes, 128), nodes)
        masked = nt(query[...], kv[rows, :head_width]) + bias[:, rows]
        new = jnp.max(masked, axis=-1, keepdims=True)
        if not first:
            new = jnp.maximum(new, top[...])
            old = jnp.exp2(top[...] - new)
        power = jnp.exp2(masked - new)
        count = jnp.sum(power, axis=-1, keepdims=True)
        summed = nn(power.astype(BF16), kv[rows, head_width:])
        norm[...] = count if first else norm[...] * old + count
        acc[...] = summed if first else acc[...] * old + summed
        top[...] = new

    shift = INDEX["sd0"] - INDEX["su0"]
    attend(1, True)
    all_passed(kv, "su", 2 - 2 * core, shift * (1 - core))
    attend(2 - 2 * core, False)
    all_passed(kv, "su", 2 * core, shift * core)
    attend(2 * core, False)

    mix_out[...] = (acc[...] / norm[...]).astype(BF16)
    mine = pl.ds(pl.multiple_of(m * head_width, 128), head_width)
    for name, q, dev in (("xr", right_m, right), ("xl", left_m, left), ("xo", opp_m, opposite)):
        send(name, rows_of(mix_out, q), mixed.at[:, mine], dev)
    mixed[:, mine] = rows_of(mix_out, m)[...]
    loads["wo"].wait()
    for i, h in enumerate((left_m, right_m, opp_m)):
        arrived("os%d" % i, wo_half(h, 1 - core))
    for name in ("xr", "xl", "xo"):
        arrived(name, mixed.at[:, mine])
    attended = nn(mixed[...], wo[...].reshape(heads * head_width, width))
    mesh_out = (own[...].astype(F32) + attended).astype(BF16)
    rows_of(md, 3)[...] = nn(mesh_out, wdec[...]).astype(BF16)

    by_place = {"own": 3, "left": 2, "right": 1, "opp": 0}

    def to_the_region_before(i, who, start, size):
        at = by_place[who]
        send("md%d" % i, rows_of(md, at, start, size), rows_of(md, at, start, size, 1), down)

    for _ in share(md, "m", by_place, lambda who, whose: by_place, to_the_region_before):
        pass

    def turned(first, count):
        return jnp.transpose(md[pl.ds(first, count), :].astype(F32)).astype(BF16)

    e2[...] += nn(turned(0, nodes), onehot[pl.ds(0, nodes), :])
    loads["whead"].wait()
    all_passed(md, "md", 1, which=range(5))
    late = -(-quarter // 128) * 128
    if late < nodes:
        e2[...] += nn(turned(nodes + late, nodes - late), onehot[pl.ds(nodes + late, nodes - late), :])
    all_passed(md, "md", 1, which=(5, 6))
    md_t[...] = turned(nodes, late)
    block = min(1024, points)
    for i in range(points // block):
        cols = slice(i * block, (i + 1) * block)
        z = e2[:, cols] + nn(md_t[...], onehot[nodes:nodes + late, cols])
        out_ref[:, cols] = nn(whead[...], silu(z).astype(BF16))

    for c in started:
        c.wait_send()


def on_device(grid_state, targets, neighbours, w_in, b_in, mesh_gain, w_qkv, w_out, w_dec, w_head):
    points, channels = grid_state.shape
    nodes, nbr = neighbours.shape
    width = w_in.shape[1]
    quarter = nodes // 4
    half = quarter // 2
    span = 3 * nodes
    heads = 4
    head_width = w_qkv.shape[2]
    out_width = w_head.shape[1]
    regions = lax.axis_size("region")
    vmem = pl.BlockSpec(memory_space=pltpu.VMEM)
    anyw = pl.BlockSpec(memory_space=pl.ANY)
    V = pltpu.VMEM
    out = pl.pallas_call(
        functools.partial(kernel, regions),
        out_shape=pltpu.VMEM((out_width, points), F32),
        in_specs=[anyw, vmem, anyw, anyw, vmem, vmem, anyw, anyw, anyw, anyw],
        out_specs=vmem,
        scratch_shapes=[
            V((channels, points), BF16), V((nbr, nodes), jnp.int32), V((channels, width), BF16),
            V((width, channels), BF16), V((width, 128), F32), V((width, 3 * head_width), BF16),
            V((heads, head_width, width), BF16), V((width, width), BF16), V((width, width), BF16),
            V((out_width, width), BF16),
            V((1, points), jnp.int32), V((nodes, nbr), jnp.int32),
            V((nodes // 8, 8 * nbr), jnp.int32), V((nodes // 8, 8 * nbr), jnp.int32),
            V((2 * nodes, points), BF16), V((width, points), BF16), V((width, points), F32),
            V((nodes, width), BF16), V((nodes, width), BF16), V((nodes, width), F32),
            V((quarter, width), BF16), V((half, width), BF16), V((half, width), BF16),
            V((2, quarter, width), BF16), V((quarter, width), BF16), V((quarter, width), BF16),
            V((nodes, width), BF16), V((nodes, head_width), BF16), V((span, 2 * head_width), BF16),
            V((nodes, span), F32), V((nodes, head_width), F32), V((nodes, 1), F32), V((nodes, 1), F32),
            V((quarter, heads * head_width), BF16), V((nodes, head_width), BF16),
            V((2 * nodes, width), BF16), V((width, -(-quarter // 128) * 128), BF16),
            pltpu.SemaphoreType.DMA((len(NAMES),)), pltpu.SemaphoreType.DMA((len(NAMES),)),
            pltpu.SemaphoreType.DMA((9,)),
        ],
        compiler_params=pltpu.CompilerParams(
            collective_id=0, has_side_effects=True, vmem_limit_bytes=56 * 1024 * 1024
        ),
        cost_estimate=pl.CostEstimate(flops=10 * 10 ** 9, bytes_accessed=4 * 10 ** 6, transcendentals=3 * 10 ** 6),
    )(
        grid_state.T, targets.reshape(1, points), neighbours.T, w_in, b_in.reshape(1, width),
        mesh_gain.reshape(1, width), w_qkv, w_out, w_dec, w_head.T,
    )
    return out.T


def solution(mesh):
    placed = (
        P(("region", "mp"), None),
        P(("region", "mp")),
        P("region", None),
        P(),
        P(),
        P(),
        P(None, None, "mp"),
        P("mp", None),
        P(),
        P(),
    )
    return jax.shard_map(
        on_device, mesh=mesh, in_specs=placed, out_specs=P(("region", "mp"), None), check_vma=False
    )
```

```python
import functools

import jax
import jax.numpy as jnp
from jax import lax
from jax.experimental import pallas as pl
from jax.experimental.pallas import tpu as pltpu
from jax.sharding import PartitionSpec as P

MESH = pl.DeviceIdType.MESH
BF16 = jnp.bfloat16
F32 = jnp.float32
LOG2_E = 1.4426950408889634
ABSENT = -1e30

NAMES = (
    *("or", "ol", "oo", "os0", "os1", "os2"),
    *("n0", "n1", "n2", "n3"),
    *("ar", "al", "br0", "br1", "bl0", "bl1"),
    *("sr0", "sr1", "sl0", "sl1", "sf0", "sf1"),
    *("su0", "su1", "su2", "su3", "su4", "su5", "su6"),
    *("sd0", "sd1", "sd2", "sd3", "sd4", "sd5", "sd6"),
    *("mr0", "mr1", "ml0", "ml1", "mf0", "mf1"),
    *("md0", "md1", "md2", "md3", "md4", "md5", "md6"),
)
INDEX = {name: i for i, name in enumerate(NAMES)}


def nt(a, b):
    return lax.dot_general(a, b, (((1,), (1,)), ((), ())), preferred_element_type=F32)


def nn(a, b):
    return jnp.dot(a, b, preferred_element_type=F32)


def silu(z):
    half = 0.5 * z
    return half + half * jnp.tanh(half)


def kernel(
    regions,
    x_hbm, targets_ref, nbr_hbm, w_in_hbm, b_ref, gain_ref, wqkv_hbm, wo_hbm, wdec_hbm, whead_hbm,
    out_ref,
    x, nbr, w_in, w_in_t, b_t, wqkv, wo, wdec, wdec_t, whead,
    rel, slots, code_hi, code_lo, onehot, embed, e2,
    send_n, recv_n, part, ra, ra_l, ra_r, rb, rb_l, rb_r,
    st, query, kv, bias, acc, top, norm, mixed, wod, from_state, last_t,
    ssem, rsem, lsem,
):
    r = lax.axis_index("region")
    m = lax.axis_index("mp")
    mps = 4
    up = (lax.rem(r + 1, regions), m)
    down = (lax.rem(r + regions - 1, regions), m)
    right_m = lax.rem(m + 1, mps)
    left_m = lax.rem(m + mps - 1, mps)
    opp_m = lax.rem(m + 2, mps)
    opposite = (r, opp_m)
    right = (r, right_m)
    left = (r, left_m)
    core = lax.rem(r, 2)
    sibling = (r + 1 - 2 * core, m)

    points = x.shape[1]
    width = embed.shape[0]
    nodes = nbr.shape[1]
    quarter = nodes // 4
    half = quarter // 2
    span = 3 * nodes
    neighbours = slots.shape[1]
    heads, head_width = wo.shape[0], wo.shape[1]

    started = []

    def send(name, src, dst, dev):
        i = INDEX[name]
        c = pltpu.make_async_remote_copy(
            src_ref=src, dst_ref=dst, send_sem=ssem.at[i], recv_sem=rsem.at[i],
            device_id=dev, device_id_type=MESH,
        )
        c.start()
        started.append(c)

    def arrived(name, dst, shift=0):
        i = INDEX[name] + shift
        pltpu.make_async_remote_copy(
            src_ref=dst, dst_ref=dst, send_sem=ssem.at[i], recv_sem=rsem.at[i],
            device_id=right, device_id_type=MESH,
        ).wait_recv()

    loads = {}
    for i, (name, src, dst) in enumerate((
        ("w_in", w_in_hbm, w_in), ("x", x_hbm, x), ("wo", wo_hbm, wo.at[m]), ("wdec", wdec_hbm, wdec), ("whead", whead_hbm, whead), ("nbr", nbr_hbm, nbr),
        *(("w%d" % j, wqkv_hbm.at[j], wqkv.at[:, pl.ds(j * head_width, head_width)]) for j in range(3)),
    )):
        loads[name] = pltpu.make_async_copy(src, dst, lsem.at[i])
        loads[name].start()

    barrier = pltpu.get_barrier_semaphore()
    for dev in (up, down, right, left, opposite):
        pl.semaphore_signal(barrier, inc=1, device_id=dev, device_id_type=MESH)

    here = r * nodes
    total = regions * nodes
    t = targets_ref[...] - here
    rel[...] = jnp.where(t < 0, t + total, t)
    b_t[...] = jnp.transpose(jnp.broadcast_to(b_ref[...], (128, width)))
    pl.semaphore_wait(barrier, 5)

    ho = head_width // 2

    def wo_half(h, which):
        return wo.at[h, pl.ds(pl.multiple_of(which * ho, 16), ho), :]

    for name, dev in (("or", right), ("ol", left), ("oo", opposite)):
        send(name, wo_hbm.at[pl.ds(pl.multiple_of(core * ho, 16), ho), :], wo_half(m, core), dev)

    loads["w_in"].wait()
    w_in_t[...] = jnp.transpose(w_in[...].astype(F32)).astype(BF16)
    loads["x"].wait()
    z = nn(w_in_t[...], x[...]) + jnp.concatenate([b_t[...]] * (points // 128), axis=1)
    embed[...] = silu(z).astype(BF16)

    order = (opp_m, right_m, left_m, m)

    def rows_of(ref, q, start=0, size=quarter, slot=0):
        return ref.at[pl.ds(pl.multiple_of(slot * nodes + q * quarter + start, 16), size)]

    def sums(slot, quarters):
        picks = []
        for q in quarters:
            first = slot * nodes + q * quarter
            ids = lax.broadcasted_iota(jnp.int32, (quarter, points), 0) + first
            picks.append((ids == rel[...]).astype(F32).astype(BF16))
            rows_of(onehot, q, slot=slot)[...] = picks[-1]
        return nt(jnp.concatenate(picks, axis=0), embed[...])

    for k in (0, 2):
        rows_of(send_n, k, 0, 2 * quarter)[...] = sums(1, order[k:k + 2]).astype(BF16)
        for i in (k, k + 1):
            send("n%d" % i, rows_of(send_n, i), rows_of(recv_n, i), up)
    part[...] = sums(0, order)

    for i, (name, h) in enumerate((("or", left_m), ("ol", right_m), ("oo", opp_m))):
        arrived(name, wo_half(h, core))
        send("os%d" % i, wo_half(h, core), wo_half(h, core), sibling)

    def both(q, start=0, size=quarter):
        return rows_of(part, q, start, size)[...] + rows_of(recv_n, q, start, size)[...].astype(F32)

    lo, hi = pl.ds(0, half), pl.ds(half, half)
    arrived("n0", rows_of(recv_n, 0))
    ra[...] = both(0).astype(BF16)
    send("ar", ra.at[lo], ra_l, right)
    send("al", ra.at[hi], ra_r, left)

    loads["nbr"].wait()
    s = jnp.transpose(nbr[...]) - (here - nodes)
    s = jnp.where(s < 0, s + total, s)
    slots[...] = jnp.where(s >= total, s - total, s)
    groups = nodes // 8
    for i in range(8):
        piece = slots[pl.ds(i, groups, stride=8), :]
        cols = slice(i * neighbours, (i + 1) * neighbours)
        code_hi[:, cols] = (piece >> 7) + i * 16
        code_lo[:, cols] = piece & 127
    together = 5 if groups % 20 == 0 else 4
    share_of_counts = groups // (4 * together)

    def count_groups(j, _):
        ids = lax.broadcasted_iota(jnp.int32, (128, 8 * neighbours), 0)
        for u in range(together):
            g = j * together + u
            high = (ids == code_hi[pl.ds(g, 1), :]).astype(F32).astype(BF16)
            low = (ids == code_lo[pl.ds(g, 1), :]).astype(F32).astype(BF16)
            count = nt(high, low)
            log = jnp.where(count > 0.0, jnp.log2(count), ABSENT).reshape(8, 16, 128)
            for c in range(span // 128):
                bias[pl.ds(pl.multiple_of(g * 8, 8), 8), c * 128:(c + 1) * 128] = log[:, c, :]
        return 0

    def counts(i):
        lax.fori_loop(i * share_of_counts, (i + 1) * share_of_counts, count_groups, 0)

    counts(0)
    counts(1)

    arrived("n1", rows_of(recv_n, 1))
    rb[0, hi] = both(1, half, half).astype(BF16)
    send("br1", rb.at[0, hi], rb_l.at[hi], right)
    arrived("ar", ra_l)
    rb[0, lo] = (both(1, 0, half) + ra_l[...].astype(F32)).astype(BF16)
    send("br0", rb.at[0, lo], rb_l.at[lo], right)
    arrived("n2", rows_of(recv_n, 2))
    rb[1, lo] = both(2, 0, half).astype(BF16)
    send("bl0", rb.at[1, lo], rb_r.at[lo], left)
    arrived("al", ra_r)
    rb[1, hi] = (both(2, half, half) + ra_r[...].astype(F32)).astype(BF16)
    send("bl1", rb.at[1, hi], rb_r.at[hi], left)
    arrived("n3", rows_of(recv_n, 3))
    for name, ref in (("br1", rb_l.at[hi]), ("br0", rb_l.at[lo]), ("bl0", rb_r.at[lo]), ("bl1", rb_r.at[hi])):
        arrived(name, ref)
    mesh_in = both(3) + rb_l[...].astype(F32) + rb_r[...].astype(F32)
    mean = jnp.mean(mesh_in * mesh_in, axis=-1, keepdims=True)
    state = (mesh_in * lax.rsqrt(mean + 1e-05) * gain_ref[...]).astype(BF16)

    def share(view, tag, size, slot, out):
        cut = size // 2

        def give(name, q, start, dev):
            send(tag + name, view(slot, q, start, cut), view(slot, q, start, cut), dev)

        def got(name, q, start):
            arrived(tag + name, view(slot, q, start, cut))

        def pass_on(i, q, start=0, count=cut):
            for name, to_slot, dev in out:
                send(name + str(i), view(slot, q, start, count), view(to_slot, q, start, count), dev)

        give("r0", m, 0, right)
        give("l1", m, cut, left)
        pass_on(0, m, 0, size)
        give("r1", m, cut, right)
        give("l0", m, 0, left)
        yield
        got("r0", left_m, 0)
        give("f0", left_m, 0, right)
        pass_on(1, left_m)
        got("l1", right_m, cut)
        give("f1", right_m, cut, left)
        pass_on(2, right_m, cut)
        yield
        got("r1", left_m, cut)
        pass_on(3, left_m, cut)
        got("l0", right_m, 0)
        pass_on(4, right_m)
        yield
        got("f0", opp_m, 0)
        pass_on(5, opp_m)
        got("f1", opp_m, cut)
        pass_on(6, opp_m, cut)
        yield

    def all_passed(view, name, slot, size, shift=0):
        for i in range(7):
            arrived(name + str(i), view(slot, 0, 0, size // 2 if i else size), shift)

    def state_view(slot, q, start, size):
        return rows_of(st, q, start, size, slot)

    state_view(1, m, 0, quarter)[...] = state
    steps = share(state_view, "s", quarter, 1, (("su", 0, up), ("sd", 2, down)))
    next(steps)
    counts(2)
    next(steps)
    counts(3)
    next(steps)

    loads["wdec"].wait()
    wdec_t[...] = jnp.transpose(wdec[...].astype(F32)).astype(BF16)
    e2[...] = nn(wdec_t[...], embed[...])
    next(steps)

    scale = LOG2_E * head_width ** -0.5
    for j in range(3):
        loads["w%d" % j].wait()

    def project(slot):
        rows = pl.ds(pl.multiple_of(slot * nodes, 128), nodes)
        if isinstance(slot, int):
            query[...] = (nn(st[rows, :], wqkv[:, :head_width]) * scale).astype(BF16)
        kv[...] = nn(st[rows, :], wqkv[:, head_width:]).astype(BF16)

    def attend(slot, first):
        project(slot)
        cols = pl.ds(pl.multiple_of(slot * nodes, 128), nodes)
        masked = nt(query[...], kv[:, :head_width]) + bias[:, cols]
        new = jnp.max(masked, axis=-1, keepdims=True)
        if not first:
            new = jnp.maximum(new, top[...])
            old = jnp.exp2(top[...] - new)
        power = jnp.exp2(masked - new)
        count = jnp.sum(power, axis=-1, keepdims=True)
        summed = nn(power.astype(BF16), kv[:, head_width:])
        norm[...] = count if first else norm[...] * old + count
        acc[...] = summed if first else acc[...] * old + summed
        top[...] = new

    shift = INDEX["sd0"] - INDEX["su0"]
    attend(1, True)
    all_passed(state_view, "su", 2 - 2 * core, quarter, shift * (1 - core))
    attend(2 - 2 * core, False)
    all_passed(state_view, "su", 2 * core, quarter, shift * core)
    attend(2 * core, False)

    def mixed_view(slot, h, start, size):
        cols = pl.ds(pl.multiple_of(h * head_width, 128), head_width)
        return mixed.at[pl.ds(slot * nodes + start, size), cols]

    mixed_view(0, m, 0, nodes)[...] = (acc[...] / norm[...]).astype(BF16)
    steps = share(mixed_view, "m", nodes, 0, (("md", 1, down),))
    next(steps)

    loads["wo"].wait()
    for i, h in enumerate((left_m, right_m, opp_m)):
        arrived("os%d" % i, wo_half(h, 1 - core))
    wod[...] = nn(wo[...].reshape(heads * head_width, width), wdec[...]).astype(BF16)
    next(steps)
    from_state[...] = nn(st[nodes:, :], wdec[...])
    next(steps)
    next(steps)

    def decoded(slot):
        rows = pl.ds(slot * nodes, nodes)
        return jnp.transpose(nn(mixed[rows, :], wod[...]) + from_state[rows, :]).astype(BF16)

    e2[...] += nn(decoded(0), onehot[pl.ds(0, nodes), :])
    loads["whead"].wait()
    all_passed(mixed_view, "md", 1, nodes)
    last_t[...] = decoded(1)
    block = min(1024, points)
    for i in range(points // block):
        cols = slice(i * block, (i + 1) * block)
        z = e2[:, cols] + nn(last_t[...], onehot[nodes:, cols])
        out_ref[:, cols] = nn(whead[...], silu(z).astype(BF16))

    for c in started:
        c.wait_send()


def on_device(grid_state, targets, neighbours, w_in, b_in, mesh_gain, w_qkv, w_out, w_dec, w_head):
    points, channels = grid_state.shape
    nodes, nbr = neighbours.shape
    width = w_in.shape[1]
    quarter = nodes // 4
    half = quarter // 2
    span = 3 * nodes
    heads = 4
    head_width = w_qkv.shape[2]
    out_width = w_head.shape[1]
    regions = lax.axis_size("region")
    vmem = pl.BlockSpec(memory_space=pltpu.VMEM)
    anyw = pl.BlockSpec(memory_space=pl.ANY)
    V = pltpu.VMEM
    out = pl.pallas_call(
        functools.partial(kernel, regions),
        out_shape=pltpu.VMEM((out_width, points), F32),
        in_specs=[anyw, vmem, anyw, anyw, vmem, vmem, anyw, anyw, anyw, anyw],
        out_specs=vmem,
        scratch_shapes=[
            V((channels, points), BF16), V((nbr, nodes), jnp.int32), V((channels, width), BF16),
            V((width, channels), BF16), V((width, 128), F32), V((width, 3 * head_width), BF16),
            V((heads, head_width, width), BF16), V((width, width), BF16), V((width, width), BF16),
            V((out_width, width), BF16),
            V((1, points), jnp.int32), V((nodes, nbr), jnp.int32),
            V((nodes // 8, 8 * nbr), jnp.int32), V((nodes // 8, 8 * nbr), jnp.int32),
            V((2 * nodes, points), BF16), V((width, points), BF16), V((width, points), F32),
            V((nodes, width), BF16), V((nodes, width), BF16), V((nodes, width), F32),
            V((quarter, width), BF16), V((half, width), BF16), V((half, width), BF16),
            V((2, quarter, width), BF16), V((quarter, width), BF16), V((quarter, width), BF16),
            V((span, width), BF16), V((nodes, head_width), BF16), V((nodes, 2 * head_width), BF16),
            V((nodes, span), F32), V((nodes, head_width), F32), V((nodes, 1), F32), V((nodes, 1), F32),
            V((2 * nodes, heads * head_width), BF16), V((heads * head_width, width), BF16),
            V((2 * nodes, width), F32), V((width, nodes), BF16),
            pltpu.SemaphoreType.DMA((len(NAMES),)), pltpu.SemaphoreType.DMA((len(NAMES),)),
            pltpu.SemaphoreType.DMA((9,)),
        ],
        compiler_params=pltpu.CompilerParams(
            collective_id=0, has_side_effects=True, vmem_limit_bytes=56 * 1024 * 1024
        ),
        cost_estimate=pl.CostEstimate(flops=10 * 10 ** 9, bytes_accessed=4 * 10 ** 6, transcendentals=3 * 10 ** 6),
    )(
        grid_state.T, targets.reshape(1, points), neighbours.T, w_in, b_in.reshape(1, width),
        mesh_gain.reshape(1, width), w_qkv, w_out, w_dec, w_head.T,
    )
    return out.T


def solution(mesh):
    placed = (
        P(("region", "mp"), None),
        P(("region", "mp")),
        P("region", None),
        P(),
        P(),
        P(),
        P(None, None, "mp"),
        P("mp", None),
        P(),
        P(),
    )
    return jax.shard_map(
        on_device, mesh=mesh, in_specs=placed, out_specs=P(("region", "mp"), None), check_vma=False
    )
```

```python
import functools

import jax
import jax.numpy as jnp
from jax import lax
from jax.experimental import pallas as pl
from jax.experimental.pallas import tpu as pltpu
from jax.sharding import PartitionSpec as P

MESH = pl.DeviceIdType.MESH
BF16 = jnp.bfloat16
F32 = jnp.float32
LOG2_E = 1.4426950408889634
ABSENT = -1e30

NAMES = (
    *("or", "ol", "oo", "os0", "os1", "os2"),
    *("n0", "n1", "n2", "n3"),
    *("ar", "al", "br0", "br1", "bl0", "bl1"),
    *("sr0", "sr1", "sr2", "sl0", "sl1", "sl2", "sf0", "sf1", "sg0", "sg1"),
    *("su%d" % i for i in range(11)),
    *("sd%d" % i for i in range(11)),
    *("mr0", "mr1", "mr2", "ml0", "ml1", "ml2", "mf0", "mf1", "mg0", "mg1"),
    *("md%d" % i for i in range(11)),
)
INDEX = {name: i for i, name in enumerate(NAMES)}


def nt(a, b):
    return lax.dot_general(a, b, (((1,), (1,)), ((), ())), preferred_element_type=F32)


def nn(a, b):
    return jnp.dot(a, b, preferred_element_type=F32)


def silu(z):
    half = 0.5 * z
    return half + half * jnp.tanh(half)


def kernel(
    regions,
    x_hbm, targets_ref, nbr_hbm, w_in_hbm, b_ref, gain_ref, wqkv_hbm, wo_hbm, wdec_hbm, whead_hbm,
    out_ref,
    x, nbr, w_in, w_in_t, b_t, wqkv, wo, wdec, wdec_t, whead,
    rel, slots, code_hi, code_lo, onehot, embed, e2,
    send_n, recv_n, part, ra, ra_l, ra_r, rb, rb_l, rb_r,
    st, query, kv, bias, acc, top, norm, mixed, wod, from_state, last_t,
    ssem, rsem, lsem,
):
    r = lax.axis_index("region")
    m = lax.axis_index("mp")
    mps = 4
    up = (lax.rem(r + 1, regions), m)
    down = (lax.rem(r + regions - 1, regions), m)
    right_m = lax.rem(m + 1, mps)
    left_m = lax.rem(m + mps - 1, mps)
    opp_m = lax.rem(m + 2, mps)
    opposite = (r, opp_m)
    right = (r, right_m)
    left = (r, left_m)
    core = lax.rem(r, 2)
    sibling = (r + 1 - 2 * core, m)

    points = x.shape[1]
    width = embed.shape[0]
    nodes = nbr.shape[1]
    quarter = nodes // 4
    half = quarter // 2
    span = 3 * nodes
    neighbours = slots.shape[1]
    heads, head_width = wo.shape[0], wo.shape[1]

    started = []

    def send(name, src, dst, dev):
        i = INDEX[name]
        c = pltpu.make_async_remote_copy(
            src_ref=src, dst_ref=dst, send_sem=ssem.at[i], recv_sem=rsem.at[i],
            device_id=dev, device_id_type=MESH,
        )
        c.start()
        started.append(c)

    def arrived(name, dst, shift=0):
        i = INDEX[name] + shift
        pltpu.make_async_remote_copy(
            src_ref=dst, dst_ref=dst, send_sem=ssem.at[i], recv_sem=rsem.at[i],
            device_id=right, device_id_type=MESH,
        ).wait_recv()

    loads = {}
    for i, (name, src, dst) in enumerate((
        ("w_in", w_in_hbm, w_in), ("x", x_hbm, x), ("wo", wo_hbm, wo.at[m]), ("wdec", wdec_hbm, wdec), ("whead", whead_hbm, whead), ("nbr", nbr_hbm, nbr),
        *(("w%d" % j, wqkv_hbm.at[j], wqkv.at[:, pl.ds(j * head_width, head_width)]) for j in range(3)),
    )):
        loads[name] = pltpu.make_async_copy(src, dst, lsem.at[i])
        loads[name].start()

    barrier = pltpu.get_barrier_semaphore()
    for dev in (up, down, right, left, opposite):
        pl.semaphore_signal(barrier, inc=1, device_id=dev, device_id_type=MESH)

    here = r * nodes
    total = regions * nodes
    t = targets_ref[...] - here
    rel[...] = jnp.where(t < 0, t + total, t)
    b_t[...] = jnp.transpose(jnp.broadcast_to(b_ref[...], (128, width)))
    pl.semaphore_wait(barrier, 5)

    ho = head_width // 2

    def wo_half(h, which):
        return wo.at[h, pl.ds(pl.multiple_of(which * ho, 16), ho), :]

    for name, dev in (("or", right), ("ol", left), ("oo", opposite)):
        send(name, wo_hbm.at[pl.ds(pl.multiple_of(core * ho, 16), ho), :], wo_half(m, core), dev)

    loads["w_in"].wait()
    w_in_t[...] = jnp.transpose(w_in[...].astype(F32)).astype(BF16)
    loads["x"].wait()
    z = nn(w_in_t[...], x[...]) + jnp.concatenate([b_t[...]] * (points // 128), axis=1)
    embed[...] = silu(z).astype(BF16)

    order = (opp_m, right_m, left_m, m)

    def rows_of(ref, q, start=0, size=quarter, slot=0):
        return ref.at[pl.ds(pl.multiple_of(slot * nodes + q * quarter + start, 16), size)]

    def sums(slot, quarters):
        picks = []
        for q in quarters:
            first = slot * nodes + q * quarter
            ids = lax.broadcasted_iota(jnp.int32, (quarter, points), 0) + first
            picks.append((ids == rel[...]).astype(F32).astype(BF16))
            rows_of(onehot, q, slot=slot)[...] = picks[-1]
        return nt(jnp.concatenate(picks, axis=0), embed[...])

    for k in (0, 2):
        rows_of(send_n, k, 0, 2 * quarter)[...] = sums(1, order[k:k + 2]).astype(BF16)
        for i in (k, k + 1):
            send("n%d" % i, rows_of(send_n, i), rows_of(recv_n, i), up)
    part[...] = sums(0, order)

    for i, (name, h) in enumerate((("or", left_m), ("ol", right_m), ("oo", opp_m))):
        arrived(name, wo_half(h, core))
        send("os%d" % i, wo_half(h, core), wo_half(h, core), sibling)

    def both(q, start=0, size=quarter):
        return rows_of(part, q, start, size)[...] + rows_of(recv_n, q, start, size)[...].astype(F32)

    lo, hi = pl.ds(0, half), pl.ds(half, half)
    arrived("n0", rows_of(recv_n, 0))
    ra[...] = both(0).astype(BF16)
    send("ar", ra.at[lo], ra_l, right)
    send("al", ra.at[hi], ra_r, left)

    loads["nbr"].wait()
    s = jnp.transpose(nbr[...]) - (here - nodes)
    s = jnp.where(s < 0, s + total, s)
    slots[...] = jnp.where(s >= total, s - total, s)
    groups = nodes // 8
    for i in range(8):
        piece = slots[pl.ds(i, groups, stride=8), :]
        cols = slice(i * neighbours, (i + 1) * neighbours)
        code_hi[:, cols] = (piece >> 7) + i * 16
        code_lo[:, cols] = piece & 127
    together = 5 if groups % 20 == 0 else 4
    share_of_counts = groups // (4 * together)

    def count_groups(j, _):
        ids = lax.broadcasted_iota(jnp.int32, (128, 8 * neighbours), 0)
        for u in range(together):
            g = j * together + u
            high = (ids == code_hi[pl.ds(g, 1), :]).astype(F32).astype(BF16)
            low = (ids == code_lo[pl.ds(g, 1), :]).astype(F32).astype(BF16)
            count = nt(high, low)
            log = jnp.where(count > 0.0, jnp.log2(count), ABSENT).reshape(8, 16, 128)
            for c in range(span // 128):
                bias[pl.ds(pl.multiple_of(g * 8, 8), 8), c * 128:(c + 1) * 128] = log[:, c, :]
        return 0

    def counts(i):
        lax.fori_loop(i * share_of_counts, (i + 1) * share_of_counts, count_groups, 0)

    counts(0)
    counts(1)

    arrived("n1", rows_of(recv_n, 1))
    rb[0, hi] = both(1, half, half).astype(BF16)
    send("br1", rb.at[0, hi], rb_l.at[hi], right)
    arrived("ar", ra_l)
    rb[0, lo] = (both(1, 0, half) + ra_l[...].astype(F32)).astype(BF16)
    send("br0", rb.at[0, lo], rb_l.at[lo], right)
    counts(2)
    arrived("n2", rows_of(recv_n, 2))
    rb[1, lo] = both(2, 0, half).astype(BF16)
    send("bl0", rb.at[1, lo], rb_r.at[lo], left)
    arrived("al", ra_r)
    rb[1, hi] = (both(2, half, half) + ra_r[...].astype(F32)).astype(BF16)
    send("bl1", rb.at[1, hi], rb_r.at[hi], left)
    counts(3)
    arrived("n3", rows_of(recv_n, 3))
    for name, ref in (("br1", rb_l.at[hi]), ("br0", rb_l.at[lo]), ("bl0", rb_r.at[lo]), ("bl1", rb_r.at[hi])):
        arrived(name, ref)
    mesh_in = both(3) + rb_l[...].astype(F32) + rb_r[...].astype(F32)
    mean = jnp.mean(mesh_in * mesh_in, axis=-1, keepdims=True)
    state = (mesh_in * lax.rsqrt(mean + 1e-05) * gain_ref[...]).astype(BF16)

    def share_pieces(size):
        cut = size // 2
        one = -(-cut // 32) * 16
        return {"0": (0, one), "1": (one, cut - one), "2": (cut, cut)}, {"0": (cut, one), "1": (cut + one, cut - one), "2": (0, cut)}

    def share(view, tag, size, slot, out):
        to_right, to_left = share_pieces(size)

        def give(name, q, piece, dev):
            send(tag + name, view(slot, q, *piece), view(slot, q, *piece), dev)

        def got(name, q, piece):
            arrived(tag + name, view(slot, q, *piece))

        def pass_on(i, q, piece):
            for name, to_slot, dev in out:
                send(name + str(i), view(slot, q, *piece), view(to_slot, q, *piece), dev)

        give("r0", m, to_right["0"], right)
        give("l0", m, to_left["0"], left)
        pass_on(0, m, (0, size))
        for k in ("1", "2"):
            give("r" + k, m, to_right[k], right)
            give("l" + k, m, to_left[k], left)
        yield
        for i, k in ((1, "0"), (3, "1")):
            got("r" + k, left_m, to_right[k])
            give("f" + k, left_m, to_right[k], right)
            pass_on(i, left_m, to_right[k])
            got("l" + k, right_m, to_left[k])
            give("g" + k, right_m, to_left[k], left)
            pass_on(i + 1, right_m, to_left[k])
        yield
        got("r2", left_m, to_right["2"])
        pass_on(5, left_m, to_right["2"])
        got("l2", right_m, to_left["2"])
        pass_on(6, right_m, to_left["2"])
        yield
        for i, k in ((7, "0"), (9, "1")):
            got("f" + k, opp_m, to_right[k])
            pass_on(i, opp_m, to_right[k])
            got("g" + k, opp_m, to_left[k])
            pass_on(i + 1, opp_m, to_left[k])
        yield

    def all_passed(view, name, slot, size, shift=0):
        pieces = share_pieces(size)[0]
        for i, k in enumerate((None, "0", "0", "1", "1", "2", "2", "0", "0", "1", "1")):
            arrived(name + str(i), view(slot, 0, 0, pieces[k][1] if k else size), shift)

    def state_view(slot, q, start, size):
        return rows_of(st, q, start, size, slot)

    state_view(1, m, 0, quarter)[...] = state
    steps = share(state_view, "s", quarter, 1, (("su", 0, up), ("sd", 2, down)))
    next(steps)
    next(steps)
    next(steps)

    loads["wdec"].wait()
    wdec_t[...] = jnp.transpose(wdec[...].astype(F32)).astype(BF16)
    e2[...] = nn(wdec_t[...], embed[...])
    next(steps)

    scale = LOG2_E * head_width ** -0.5
    for j in range(3):
        loads["w%d" % j].wait()

    def project(slot):
        rows = pl.ds(pl.multiple_of(slot * nodes, 128), nodes)
        if isinstance(slot, int):
            query[...] = (nn(st[rows, :], wqkv[:, :head_width]) * scale).astype(BF16)
        kv[...] = nn(st[rows, :], wqkv[:, head_width:]).astype(BF16)

    def attend(slot, first):
        project(slot)
        cols = pl.ds(pl.multiple_of(slot * nodes, 128), nodes)
        masked = nt(query[...], kv[:, :head_width]) + bias[:, cols]
        new = jnp.max(masked, axis=-1, keepdims=True)
        if not first:
            new = jnp.maximum(new, top[...])
            old = jnp.exp2(top[...] - new)
        power = jnp.exp2(masked - new)
        count = jnp.sum(power, axis=-1, keepdims=True)
        summed = nn(power.astype(BF16), kv[:, head_width:])
        norm[...] = count if first else norm[...] * old + count
        acc[...] = summed if first else acc[...] * old + summed
        top[...] = new

    shift = INDEX["sd0"] - INDEX["su0"]
    attend(1, True)
    all_passed(state_view, "su", 2 - 2 * core, quarter, shift * (1 - core))
    attend(2 - 2 * core, False)
    all_passed(state_view, "su", 2 * core, quarter, shift * core)
    attend(2 * core, False)

    def mixed_view(slot, h, start, size):
        cols = pl.ds(pl.multiple_of(h * head_width, 128), head_width)
        return mixed.at[pl.ds(slot * nodes + start, size), cols]

    mixed_view(0, m, 0, nodes)[...] = (acc[...] / norm[...]).astype(BF16)
    steps = share(mixed_view, "m", nodes, 0, (("md", 1, down),))
    next(steps)

    loads["wo"].wait()
    for i, h in enumerate((left_m, right_m, opp_m)):
        arrived("os%d" % i, wo_half(h, 1 - core))
    wod[...] = nn(wo[...].reshape(heads * head_width, width), wdec[...]).astype(BF16)
    next(steps)
    from_state[...] = nn(st[nodes:, :], wdec[...])
    next(steps)
    next(steps)

    def decoded(slot):
        rows = pl.ds(slot * nodes, nodes)
        return jnp.transpose(nn(mixed[rows, :], wod[...]) + from_state[rows, :]).astype(BF16)

    e2[...] += nn(decoded(0), onehot[pl.ds(0, nodes), :])
    loads["whead"].wait()
    all_passed(mixed_view, "md", 1, nodes)
    last_t[...] = decoded(1)
    block = min(1024, points)
    for i in range(points // block):
        cols = slice(i * block, (i + 1) * block)
        z = e2[:, cols] + nn(last_t[...], onehot[nodes:, cols])
        out_ref[:, cols] = nn(whead[...], silu(z).astype(BF16))

    for c in started:
        c.wait_send()


def on_device(grid_state, targets, neighbours, w_in, b_in, mesh_gain, w_qkv, w_out, w_dec, w_head):
    points, channels = grid_state.shape
    nodes, nbr = neighbours.shape
    width = w_in.shape[1]
    quarter = nodes // 4
    half = quarter // 2
    span = 3 * nodes
    heads = 4
    head_width = w_qkv.shape[2]
    out_width = w_head.shape[1]
    regions = lax.axis_size("region")
    vmem = pl.BlockSpec(memory_space=pltpu.VMEM)
    anyw = pl.BlockSpec(memory_space=pl.ANY)
    V = pltpu.VMEM
    out = pl.pallas_call(
        functools.partial(kernel, regions),
        out_shape=pltpu.VMEM((out_width, points), F32),
        in_specs=[anyw, vmem, anyw, anyw, vmem, vmem, anyw, anyw, anyw, anyw],
        out_specs=vmem,
        scratch_shapes=[
            V((channels, points), BF16), V((nbr, nodes), jnp.int32), V((channels, width), BF16),
            V((width, channels), BF16), V((width, 128), F32), V((width, 3 * head_width), BF16),
            V((heads, head_width, width), BF16), V((width, width), BF16), V((width, width), BF16),
            V((out_width, width), BF16),
            V((1, points), jnp.int32), V((nodes, nbr), jnp.int32),
            V((nodes // 8, 8 * nbr), jnp.int32), V((nodes // 8, 8 * nbr), jnp.int32),
            V((2 * nodes, points), BF16), V((width, points), BF16), V((width, points), F32),
            V((nodes, width), BF16), V((nodes, width), BF16), V((nodes, width), F32),
            V((quarter, width), BF16), V((half, width), BF16), V((half, width), BF16),
            V((2, quarter, width), BF16), V((quarter, width), BF16), V((quarter, width), BF16),
            V((span, width), BF16), V((nodes, head_width), BF16), V((nodes, 2 * head_width), BF16),
            V((nodes, span), F32), V((nodes, head_width), F32), V((nodes, 1), F32), V((nodes, 1), F32),
            V((2 * nodes, heads * head_width), BF16), V((heads * head_width, width), BF16),
            V((2 * nodes, width), F32), V((width, nodes), BF16),
            pltpu.SemaphoreType.DMA((len(NAMES),)), pltpu.SemaphoreType.DMA((len(NAMES),)),
            pltpu.SemaphoreType.DMA((9,)),
        ],
        compiler_params=pltpu.CompilerParams(
            collective_id=0, has_side_effects=True, vmem_limit_bytes=56 * 1024 * 1024
        ),
        cost_estimate=pl.CostEstimate(flops=10 * 10 ** 9, bytes_accessed=4 * 10 ** 6, transcendentals=3 * 10 ** 6),
    )(
        grid_state.T, targets.reshape(1, points), neighbours.T, w_in, b_in.reshape(1, width),
        mesh_gain.reshape(1, width), w_qkv, w_out, w_dec, w_head.T,
    )
    return out.T


def solution(mesh):
    placed = (
        P(("region", "mp"), None),
        P(("region", "mp")),
        P("region", None),
        P(),
        P(),
        P(),
        P(None, None, "mp"),
        P("mp", None),
        P(),
        P(),
    )
    return jax.shard_map(
        on_device, mesh=mesh, in_specs=placed, out_specs=P(("region", "mp"), None), check_vma=False
    )
```

```python
import functools

import jax
import jax.numpy as jnp
from jax import lax
from jax.experimental import pallas as pl
from jax.experimental.pallas import tpu as pltpu
from jax.sharding import PartitionSpec as P

MESH = pl.DeviceIdType.MESH
BF16 = jnp.bfloat16
F32 = jnp.float32
LOG2_E = 1.4426950408889634
ABSENT = -1e30

NAMES = (
    *("or", "ol", "oo", "os0", "os1", "os2"),
    *("n0", "n1", "n2", "n3"),
    *("ar", "al", "br0", "br1", "bl0", "bl1"),
    *("sr0", "sr1", "sl0", "sl1", "sf0", "sf1"),
    *("su0", "su1", "su2", "su3", "su4", "su5", "su6"),
    *("sd0", "sd1", "sd2", "sd3", "sd4", "sd5", "sd6"),
    *("mr0", "mr1", "ml0", "ml1", "mf0", "mf1"),
    *("md0", "md1", "md2", "md3", "md4", "md5", "md6"),
)
INDEX = {name: i for i, name in enumerate(NAMES)}


def nt(a, b):
    return lax.dot_general(a, b, (((1,), (1,)), ((), ())), preferred_element_type=F32)


def nn(a, b):
    return jnp.dot(a, b, preferred_element_type=F32)


def silu(z):
    half = 0.5 * z
    return half + half * jnp.tanh(half)


def kernel(
    regions,
    x_hbm, targets_hbm, nbr_hbm, w_in_hbm, b_hbm, gain_hbm, wqkv_hbm, wo_hbm, wdec_hbm, whead_hbm,
    out_ref,
    x, targets, nbr, w_in, b_in, gain, w_in_t, b_t, wqkv, wo, wdec, wdec_t, whead,
    rel, slots, code_hi, code_lo, onehot, embed, e2,
    send_n, recv_n, part, ra, ra_l, ra_r, rb, rb_l, rb_r,
    st, query, kv, bias, acc, top, norm, mixed, wod, from_state, last_t,
    ssem, rsem, lsem,
):
    r = lax.axis_index("region")
    m = lax.axis_index("mp")
    mps = 4
    up = (lax.rem(r + 1, regions), m)
    down = (lax.rem(r + regions - 1, regions), m)
    right_m = lax.rem(m + 1, mps)
    left_m = lax.rem(m + mps - 1, mps)
    opp_m = lax.rem(m + 2, mps)
    opposite = (r, opp_m)
    right = (r, right_m)
    left = (r, left_m)
    core = lax.rem(r, 2)
    sibling = (r + 1 - 2 * core, m)

    points = x.shape[1]
    width = embed.shape[0]
    nodes = nbr.shape[1]
    quarter = nodes // 4
    half = quarter // 2
    span = 3 * nodes
    neighbours = slots.shape[1]
    heads, head_width = wo.shape[0], wo.shape[1]

    started = []

    def send(name, src, dst, dev, shift=0):
        i = INDEX[name] + shift
        c = pltpu.make_async_remote_copy(
            src_ref=src, dst_ref=dst, send_sem=ssem.at[i], recv_sem=rsem.at[i],
            device_id=dev, device_id_type=MESH,
        )
        c.start()
        started.append(c)

    def sent():
        for c in started:
            c.wait_send()
        started.clear()

    def arrived(name, dst, shift=0):
        i = INDEX[name] + shift
        pltpu.make_async_remote_copy(
            src_ref=dst, dst_ref=dst, send_sem=ssem.at[i], recv_sem=rsem.at[i],
            device_id=right, device_id_type=MESH,
        ).wait_recv()

    loads = {}
    for i, (name, src, dst) in enumerate((
        ("w_in", w_in_hbm, w_in), ("x", x_hbm, x), ("b", b_hbm, b_in), ("targets", targets_hbm, targets), ("gain", gain_hbm, gain), ("wo", wo_hbm, wo.at[m]), ("wdec", wdec_hbm, wdec), ("whead", whead_hbm, whead), ("nbr", nbr_hbm, nbr),
        *(("w%d" % j, wqkv_hbm.at[j], wqkv.at[:, pl.ds(j * head_width, head_width)]) for j in range(3)),
    )):
        loads[name] = pltpu.make_async_copy(src, dst, lsem.at[i])
        loads[name].start()

    barrier = pltpu.get_barrier_semaphore()
    for dev in (up, down, right, left, opposite):
        pl.semaphore_signal(barrier, inc=1, device_id=dev, device_id_type=MESH)

    here = r * nodes
    total = regions * nodes
    loads["w_in"].wait()
    w_in_t[...] = jnp.transpose(w_in[...].astype(F32)).astype(BF16)
    loads["b"].wait()
    b_t[...] = jnp.transpose(jnp.broadcast_to(b_in[...], (128, width)))
    loads["targets"].wait()
    t = targets[...] - here
    rel[...] = jnp.where(t < 0, t + total, t)

    loads["x"].wait()
    z = nn(w_in_t[...], x[...]) + jnp.concatenate([b_t[...]] * (points // 128), axis=1)
    embed[...] = silu(z).astype(BF16)

    pl.semaphore_wait(barrier, 5)

    ho = head_width // 2

    def wo_half(h, which):
        return wo.at[h, pl.ds(pl.multiple_of(which * ho, 16), ho), :]

    for name, dev in (("or", right), ("ol", left), ("oo", opposite)):
        send(name, wo_hbm.at[pl.ds(pl.multiple_of(core * ho, 16), ho), :], wo_half(m, core), dev)

    order = (opp_m, right_m, left_m, m)

    def rows_of(ref, q, start=0, size=quarter, slot=0):
        return ref.at[pl.ds(pl.multiple_of(slot * nodes + q * quarter + start, 16), size)]

    def sums(slot, quarters):
        picks = []
        for q in quarters:
            first = slot * nodes + q * quarter
            ids = lax.broadcasted_iota(jnp.int32, (quarter, points), 0) + first
            picks.append((ids == rel[...]).astype(F32).astype(BF16))
            rows_of(onehot, q, slot=slot)[...] = picks[-1]
        return nt(jnp.concatenate(picks, axis=0), embed[...])

    for k in (0, 2):
        rows_of(send_n, k, 0, 2 * quarter)[...] = sums(1, order[k:k + 2]).astype(BF16)
        for i in (k, k + 1):
            send("n%d" % i, rows_of(send_n, i), rows_of(recv_n, i), up)
    part[...] = sums(0, order)

    for i, (name, h) in enumerate((("or", left_m), ("ol", right_m), ("oo", opp_m))):
        arrived(name, wo_half(h, core))
        send("os%d" % i, wo_half(h, core), wo_half(h, core), sibling)

    def both(q, start=0, size=quarter):
        return rows_of(part, q, start, size)[...] + rows_of(recv_n, q, start, size)[...].astype(F32)

    lo, hi = pl.ds(0, half), pl.ds(half, half)
    arrived("n0", rows_of(recv_n, 0))
    ra[...] = both(0).astype(BF16)
    send("ar", ra.at[lo], ra_l, right)
    send("al", ra.at[hi], ra_r, left)

    loads["nbr"].wait()
    s = jnp.transpose(nbr[...]) - (here - nodes)
    s = jnp.where(s < 0, s + total, s)
    slots[...] = jnp.where(s >= total, s - total, s)
    groups = nodes // 8
    for i in range(8):
        piece = slots[pl.ds(i, groups, stride=8), :]
        cols = slice(i * neighbours, (i + 1) * neighbours)
        code_hi[:, cols] = (piece >> 7) + i * 16
        code_lo[:, cols] = piece & 127
    together = 5 if groups % 20 == 0 else 4
    share_of_counts = groups // (4 * together)

    def count_groups(j, _):
        ids = lax.broadcasted_iota(jnp.int32, (128, 8 * neighbours), 0)
        for u in range(together):
            g = j * together + u
            high = (ids == code_hi[pl.ds(g, 1), :]).astype(F32).astype(BF16)
            low = (ids == code_lo[pl.ds(g, 1), :]).astype(F32).astype(BF16)
            count = nt(high, low)
            log = jnp.where(count > 0.0, jnp.log2(count), ABSENT).reshape(8, 16, 128)
            for c in range(span // 128):
                bias[pl.ds(pl.multiple_of(g * 8, 8), 8), c * 128:(c + 1) * 128] = log[:, c, :]
        return 0

    def counts(i):
        lax.fori_loop(i * share_of_counts, (i + 1) * share_of_counts, count_groups, 0)


    arrived("n1", rows_of(recv_n, 1))
    rb[0, hi] = both(1, half, half).astype(BF16)
    send("br1", rb.at[0, hi], rb_l.at[hi], right)
    arrived("ar", ra_l)
    rb[0, lo] = (both(1, 0, half) + ra_l[...].astype(F32)).astype(BF16)
    send("br0", rb.at[0, lo], rb_l.at[lo], right)
    arrived("n2", rows_of(recv_n, 2))
    rb[1, lo] = both(2, 0, half).astype(BF16)
    send("bl0", rb.at[1, lo], rb_r.at[lo], left)
    arrived("al", ra_r)
    rb[1, hi] = (both(2, half, half) + ra_r[...].astype(F32)).astype(BF16)
    send("bl1", rb.at[1, hi], rb_r.at[hi], left)
    arrived("n3", rows_of(recv_n, 3))
    for name, ref in (("br1", rb_l.at[hi]), ("br0", rb_l.at[lo]), ("bl0", rb_r.at[lo]), ("bl1", rb_r.at[hi])):
        arrived(name, ref)
    mesh_in = both(3) + rb_l[...].astype(F32) + rb_r[...].astype(F32)
    loads["gain"].wait()
    mean = jnp.mean(mesh_in * mesh_in, axis=-1, keepdims=True)
    state = (mesh_in * lax.rsqrt(mean + 1e-05) * gain[...]).astype(BF16)

    def share(view, tag, size, slot, out):
        cut = size // 2

        def give(name, q, start, dev):
            send(tag + name, view(slot, q, start, cut), view(slot, q, start, cut), dev)

        def got(name, q, start):
            arrived(tag + name, view(slot, q, start, cut))

        def pass_on(i, q, start=0, count=cut):
            for name, to_slot, dev, shift in out:
                send(name + str(i), view(slot, q, start, count), view(to_slot, q, start, count), dev, shift)

        give("r0", m, 0, right)
        give("l1", m, cut, left)
        pass_on(0, m, 0, size)
        give("r1", m, cut, right)
        give("l0", m, 0, left)
        yield
        got("r0", left_m, 0)
        give("f0", left_m, 0, right)
        pass_on(1, left_m)
        got("l1", right_m, cut)
        give("f1", right_m, cut, left)
        pass_on(2, right_m, cut)
        yield
        got("r1", left_m, cut)
        pass_on(3, left_m, cut)
        got("l0", right_m, 0)
        pass_on(4, right_m)
        yield
        got("f0", opp_m, 0)
        pass_on(5, opp_m)
        got("f1", opp_m, cut)
        pass_on(6, opp_m, cut)
        yield

    def all_passed(view, name, slot, size, shift=0):
        for i in range(7):
            arrived(name + str(i), view(slot, 0, 0, size // 2 if i else size), shift)

    def state_view(slot, q, start, size):
        return rows_of(st, q, start, size, slot)

    shift = INDEX["sd0"] - INDEX["su0"]
    far = "su", 2 - 2 * core, (lax.rem(r + regions - 1 + 2 * core, regions), m)
    near = "su", 2 * core, sibling
    state_view(1, m, 0, quarter)[...] = state
    steps = share(state_view, "s", quarter, 1, ((*far, shift * (1 - core)), (*near, shift * core)))
    next(steps)
    counts(0)
    counts(1)
    next(steps)
    counts(2)
    next(steps)
    counts(3)

    next(steps)

    scale = LOG2_E * head_width ** -0.5
    for j in range(3):
        loads["w%d" % j].wait()

    def project(slot):
        rows = pl.ds(pl.multiple_of(slot * nodes, 128), nodes)
        if isinstance(slot, int):
            query[...] = (nn(st[rows, :], wqkv[:, :head_width]) * scale).astype(BF16)
        kv[...] = nn(st[rows, :], wqkv[:, head_width:]).astype(BF16)

    def attend(slot, first):
        project(slot)
        cols = pl.ds(pl.multiple_of(slot * nodes, 128), nodes)
        masked = nt(query[...], kv[:, :head_width]) + bias[:, cols]
        new = jnp.max(masked, axis=-1, keepdims=True)
        if not first:
            new = jnp.maximum(new, top[...])
            old = jnp.exp2(top[...] - new)
        power = jnp.exp2(masked - new)
        count = jnp.sum(power, axis=-1, keepdims=True)
        summed = nn(power.astype(BF16), kv[:, head_width:])
        norm[...] = count if first else norm[...] * old + count
        acc[...] = summed if first else acc[...] * old + summed
        top[...] = new

    attend(1, True)
    all_passed(state_view, "su", 2 - 2 * core, quarter, shift * (1 - core))
    attend(2 - 2 * core, False)
    all_passed(state_view, "su", 2 * core, quarter, shift * core)
    attend(2 * core, False)

    def mixed_view(slot, h, start, size):
        cols = pl.ds(pl.multiple_of(h * head_width, 128), head_width)
        return mixed.at[pl.ds(slot * nodes + start, size), cols]

    mixed_view(0, m, 0, nodes)[...] = (acc[...] / norm[...]).astype(BF16)
    steps = share(mixed_view, "m", nodes, 0, (("md", 1, down, 0),))
    next(steps)

    loads["wo"].wait()
    for i, h in enumerate((left_m, right_m, opp_m)):
        arrived("os%d" % i, wo_half(h, 1 - core))
    loads["wdec"].wait()
    wod[...] = nn(wo[...].reshape(heads * head_width, width), wdec[...]).astype(BF16)
    from_state[...] = nn(st[nodes:, :], wdec[...])

    wdec_t[...] = jnp.transpose(wdec[...].astype(F32)).astype(BF16)
    e2[...] = nn(wdec_t[...], embed[...])
    next(steps)
    next(steps)
    next(steps)

    def decoded(slot):
        rows = pl.ds(slot * nodes, nodes)
        return jnp.transpose(nn(mixed[rows, :], wod[...]) + from_state[rows, :]).astype(BF16)

    e2[...] += nn(decoded(0), onehot[pl.ds(0, nodes), :])
    loads["whead"].wait()
    sent()
    all_passed(mixed_view, "md", 1, nodes)
    last_t[...] = decoded(1)
    block = points
    for i in range(points // block):
        cols = slice(i * block, (i + 1) * block)
        z = e2[:, cols] + nn(last_t[...], onehot[nodes:, cols])
        out_ref[:, cols] = nn(whead[...], silu(z).astype(BF16))

    sent()


def on_device(grid_state, targets, neighbours, w_in, b_in, mesh_gain, w_qkv, w_out, w_dec, w_head):
    points, channels = grid_state.shape
    nodes, nbr = neighbours.shape
    width = w_in.shape[1]
    quarter = nodes // 4
    half = quarter // 2
    span = 3 * nodes
    heads = 4
    head_width = w_qkv.shape[2]
    out_width = w_head.shape[1]
    regions = lax.axis_size("region")
    vmem = pl.BlockSpec(memory_space=pltpu.VMEM)
    anyw = pl.BlockSpec(memory_space=pl.ANY)
    V = pltpu.VMEM
    out = pl.pallas_call(
        functools.partial(kernel, regions),
        out_shape=pltpu.VMEM((out_width, points), F32),
        in_specs=[anyw] * 10,
        out_specs=vmem,
        scratch_shapes=[
            V((channels, points), BF16), V((1, points), jnp.int32), V((nbr, nodes), jnp.int32), V((channels, width), BF16),
            V((1, width), F32), V((1, width), F32),
            V((width, channels), BF16), V((width, 128), F32), V((width, 3 * head_width), BF16),
            V((heads, head_width, width), BF16), V((width, width), BF16), V((width, width), BF16),
            V((out_width, width), BF16),
            V((1, points), jnp.int32), V((nodes, nbr), jnp.int32),
            V((nodes // 8, 8 * nbr), jnp.int32), V((nodes // 8, 8 * nbr), jnp.int32),
            V((2 * nodes, points), BF16), V((width, points), BF16), V((width, points), F32),
            V((nodes, width), BF16), V((nodes, width), BF16), V((nodes, width), F32),
            V((quarter, width), BF16), V((half, width), BF16), V((half, width), BF16),
            V((2, quarter, width), BF16), V((quarter, width), BF16), V((quarter, width), BF16),
            V((span, width), BF16), V((nodes, head_width), BF16), V((nodes, 2 * head_width), BF16),
            V((nodes, span), F32), V((nodes, head_width), F32), V((nodes, 1), F32), V((nodes, 1), F32),
            V((2 * nodes, heads * head_width), BF16), V((heads * head_width, width), BF16),
            V((2 * nodes, width), F32), V((width, nodes), BF16),
            pltpu.SemaphoreType.DMA((len(NAMES),)), pltpu.SemaphoreType.DMA((len(NAMES),)),
            pltpu.SemaphoreType.DMA((12,)),
        ],
        compiler_params=pltpu.CompilerParams(
            collective_id=0, has_side_effects=True, vmem_limit_bytes=56 * 1024 * 1024
        ),
        cost_estimate=pl.CostEstimate(flops=10 * 10 ** 9, bytes_accessed=4 * 10 ** 6, transcendentals=3 * 10 ** 6),
    )(
        grid_state.T, targets.reshape(1, points), neighbours.T, w_in, b_in.reshape(1, width),
        mesh_gain.reshape(1, width), w_qkv, w_out, w_dec, w_head.T,
    )
    return out.T


def solution(mesh):
    placed = (
        P(("region", "mp"), None),
        P(("region", "mp")),
        P("region", None),
        P(),
        P(),
        P(),
        P(None, None, "mp"),
        P("mp", None),
        P(),
        P(),
    )
    return jax.shard_map(
        on_device, mesh=mesh, in_specs=placed, out_specs=P(("region", "mp"), None), check_vma=False
    )
```

```python
import functools

import jax
import jax.numpy as jnp
from jax import lax
from jax.experimental import pallas as pl
from jax.experimental.pallas import tpu as pltpu
from jax.sharding import PartitionSpec as P

MESH = pl.DeviceIdType.MESH
BF16 = jnp.bfloat16
F32 = jnp.float32
LOG2_E = 1.4426950408889634
ABSENT = -1e30

NAMES = (
    *("or", "ol", "oo", "os0", "os1", "os2"),
    *("n0", "n1", "n2", "n3"),
    *("ar", "al", "br0", "br1", "bl0", "bl1"),
    *("sr0", "sr1", "sl0", "sl1", "sf0", "sf1"),
    *("su0", "su1", "su2", "su3", "su4", "su5", "su6"),
    *("sd0", "sd1", "sd2", "sd3", "sd4", "sd5", "sd6"),
    *("mr0", "mr1", "ml0", "ml1", "mf0", "mf1"),
    *("md0", "md1", "md2", "md3", "md4", "md5", "md6"),
)
INDEX = {name: i for i, name in enumerate(NAMES)}


def nt(a, b):
    return lax.dot_general(a, b, (((1,), (1,)), ((), ())), preferred_element_type=F32)


def nn(a, b):
    return jnp.dot(a, b, preferred_element_type=F32)


def silu(z):
    half = 0.5 * z
    return half + half * jnp.tanh(half)


def kernel(
    regions,
    x_hbm, targets_hbm, nbr_hbm, w_in_hbm, b_hbm, gain_hbm, wqkv_hbm, wo_hbm, wdec_hbm, whead_hbm,
    out_ref,
    x, targets, nbr, w_in, b_in, gain, w_in_t, b_t, wqkv, wo, wdec, wdec_t, whead,
    rel, slots, code_hi, code_lo, onehot, embed, e2,
    send_n, recv_n, part, ra, ra_l, ra_r, rb, rb_l, rb_r,
    st, query, kv, bias, acc, top, norm, mixed, wod, from_state, last_t,
    ssem, rsem, lsem,
):
    r = lax.axis_index("region")
    m = lax.axis_index("mp")
    mps = 4
    up = (lax.rem(r + 1, regions), m)
    down = (lax.rem(r + regions - 1, regions), m)
    right_m = lax.rem(m + 1, mps)
    left_m = lax.rem(m + mps - 1, mps)
    opp_m = lax.rem(m + 2, mps)
    opposite = (r, opp_m)
    right = (r, right_m)
    left = (r, left_m)
    core = lax.rem(r, 2)
    sibling = (r + 1 - 2 * core, m)

    points = x.shape[1]
    width = embed.shape[0]
    nodes = nbr.shape[1]
    quarter = nodes // 4
    half = quarter // 2
    span = 3 * nodes
    neighbours = slots.shape[1]
    heads, head_width = wo.shape[0], wo.shape[1]

    started = []

    def send(name, src, dst, dev, shift=0):
        i = INDEX[name] + shift
        c = pltpu.make_async_remote_copy(
            src_ref=src, dst_ref=dst, send_sem=ssem.at[i], recv_sem=rsem.at[i],
            device_id=dev, device_id_type=MESH,
        )
        c.start()
        started.append(c)

    def sent():
        for c in started:
            c.wait_send()
        started.clear()

    def arrived(name, dst, shift=0):
        i = INDEX[name] + shift
        pltpu.make_async_remote_copy(
            src_ref=dst, dst_ref=dst, send_sem=ssem.at[i], recv_sem=rsem.at[i],
            device_id=right, device_id_type=MESH,
        ).wait_recv()

    loads = {}
    for i, (name, src, dst) in enumerate((
        ("w_in", w_in_hbm, w_in), ("x", x_hbm, x), ("b", b_hbm, b_in), ("targets", targets_hbm, targets), ("gain", gain_hbm, gain), ("wo", wo_hbm, wo.at[m]), ("wdec", wdec_hbm, wdec), ("whead", whead_hbm, whead), ("nbr", nbr_hbm, nbr),
        *(("w%d" % j, wqkv_hbm.at[j], wqkv.at[:, pl.ds(j * head_width, head_width)]) for j in range(3)),
    )):
        loads[name] = pltpu.make_async_copy(src, dst, lsem.at[i])
        loads[name].start()

    barrier = pltpu.get_barrier_semaphore()
    for dev in (up, down, right, left, opposite):
        pl.semaphore_signal(barrier, inc=1, device_id=dev, device_id_type=MESH)

    here = r * nodes
    total = regions * nodes
    loads["w_in"].wait()
    w_in_t[...] = jnp.transpose(w_in[...].astype(F32)).astype(BF16)
    loads["b"].wait()
    b_t[...] = jnp.transpose(jnp.broadcast_to(b_in[...], (128, width)))
    loads["targets"].wait()
    t = targets[...] - here
    rel[...] = jnp.where(t < 0, t + total, t)

    loads["x"].wait()
    z = nn(w_in_t[...], x[...]) + jnp.concatenate([b_t[...]] * (points // 128), axis=1)
    embed[...] = silu(z).astype(BF16)

    pl.semaphore_wait(barrier, 5)

    ho = head_width // 2

    def wo_half(h, which):
        return wo.at[h, pl.ds(pl.multiple_of(which * ho, 16), ho), :]

    for name, dev in (("or", right), ("ol", left), ("oo", opposite)):
        send(name, wo_hbm.at[pl.ds(pl.multiple_of(core * ho, 16), ho), :], wo_half(m, core), dev)

    order = (opp_m, right_m, left_m, m)

    def rows_of(ref, q, start=0, size=quarter, slot=0):
        return ref.at[pl.ds(pl.multiple_of(slot * nodes + q * quarter + start, 16), size)]

    def sums(slot, quarters):
        picks = []
        for q in quarters:
            first = slot * nodes + q * quarter
            ids = lax.broadcasted_iota(jnp.int32, (quarter, points), 0) + first
            picks.append((ids == rel[...]).astype(F32).astype(BF16))
            rows_of(onehot, q, slot=slot)[...] = picks[-1]
        return nt(jnp.concatenate(picks, axis=0), embed[...])

    for k in (0, 2):
        rows_of(send_n, k, 0, 2 * quarter)[...] = sums(1, order[k:k + 2]).astype(BF16)
        for i in (k, k + 1):
            send("n%d" % i, rows_of(send_n, i), rows_of(recv_n, i), up)
    part[...] = sums(0, order)

    def both(q, start=0, size=quarter):
        return rows_of(part, q, start, size)[...] + rows_of(recv_n, q, start, size)[...].astype(F32)

    lo, hi = pl.ds(0, half), pl.ds(half, half)
    arrived("n0", rows_of(recv_n, 0))
    ra[...] = both(0).astype(BF16)
    send("ar", ra.at[lo], ra_l, right)
    send("al", ra.at[hi], ra_r, left)

    loads["nbr"].wait()
    s = jnp.transpose(nbr[...]) - (here - nodes)
    s = jnp.where(s < 0, s + total, s)
    slots[...] = jnp.where(s >= total, s - total, s)
    groups = nodes // 8
    for i in range(8):
        piece = slots[pl.ds(i, groups, stride=8), :]
        cols = slice(i * neighbours, (i + 1) * neighbours)
        code_hi[:, cols] = (piece >> 7) + i * 16
        code_lo[:, cols] = piece & 127
    together = 5 if groups % 20 == 0 else 4
    share_of_counts = groups // (4 * together)

    def count_groups(j, _):
        ids = lax.broadcasted_iota(jnp.int32, (128, 8 * neighbours), 0)
        for u in range(together):
            g = j * together + u
            high = (ids == code_hi[pl.ds(g, 1), :]).astype(F32).astype(BF16)
            low = (ids == code_lo[pl.ds(g, 1), :]).astype(F32).astype(BF16)
            count = nt(high, low)
            log = jnp.where(count > 0.0, jnp.log2(count), ABSENT).reshape(8, 16, 128)
            for c in range(span // 128):
                bias[pl.ds(pl.multiple_of(g * 8, 8), 8), c * 128:(c + 1) * 128] = log[:, c, :]
        return 0

    def counts(i):
        lax.fori_loop(i * share_of_counts, (i + 1) * share_of_counts, count_groups, 0)


    counts(0)
    arrived("n1", rows_of(recv_n, 1))
    rb[0, hi] = both(1, half, half).astype(BF16)
    send("br1", rb.at[0, hi], rb_l.at[hi], right)
    arrived("ar", ra_l)
    rb[0, lo] = (both(1, 0, half) + ra_l[...].astype(F32)).astype(BF16)
    send("br0", rb.at[0, lo], rb_l.at[lo], right)
    arrived("n2", rows_of(recv_n, 2))
    rb[1, lo] = both(2, 0, half).astype(BF16)
    send("bl0", rb.at[1, lo], rb_r.at[lo], left)
    arrived("al", ra_r)
    rb[1, hi] = (both(2, half, half) + ra_r[...].astype(F32)).astype(BF16)
    send("bl1", rb.at[1, hi], rb_r.at[hi], left)
    arrived("n3", rows_of(recv_n, 3))
    for name, ref in (("br1", rb_l.at[hi]), ("br0", rb_l.at[lo]), ("bl0", rb_r.at[lo]), ("bl1", rb_r.at[hi])):
        arrived(name, ref)
    mesh_in = both(3) + rb_l[...].astype(F32) + rb_r[...].astype(F32)
    loads["gain"].wait()
    mean = jnp.mean(mesh_in * mesh_in, axis=-1, keepdims=True)
    state = (mesh_in * lax.rsqrt(mean + 1e-05) * gain[...]).astype(BF16)

    def share(view, tag, size, slot, out):
        cut = size // 2

        def give(name, q, start, dev):
            send(tag + name, view(slot, q, start, cut), view(slot, q, start, cut), dev)

        def got(name, q, start):
            arrived(tag + name, view(slot, q, start, cut))

        def pass_on(i, q, start=0, count=cut):
            for name, to_slot, dev, shift in out:
                send(name + str(i), view(slot, q, start, count), view(to_slot, q, start, count), dev, shift)

        give("r0", m, 0, right)
        give("l1", m, cut, left)
        pass_on(0, m, 0, size)
        give("r1", m, cut, right)
        give("l0", m, 0, left)
        yield
        got("r0", left_m, 0)
        give("f0", left_m, 0, right)
        pass_on(1, left_m)
        got("l1", right_m, cut)
        give("f1", right_m, cut, left)
        pass_on(2, right_m, cut)
        yield
        got("r1", left_m, cut)
        pass_on(3, left_m, cut)
        got("l0", right_m, 0)
        pass_on(4, right_m)
        yield
        got("f0", opp_m, 0)
        pass_on(5, opp_m)
        got("f1", opp_m, cut)
        pass_on(6, opp_m, cut)
        yield

    def all_passed(view, name, slot, size, shift=0):
        for i in range(7):
            arrived(name + str(i), view(slot, 0, 0, size // 2 if i else size), shift)

    def state_view(slot, q, start, size):
        return rows_of(st, q, start, size, slot)

    shift = INDEX["sd0"] - INDEX["su0"]
    far = "su", 2 - 2 * core, (lax.rem(r + regions - 1 + 2 * core, regions), m)
    near = "su", 2 * core, sibling
    state_view(1, m, 0, quarter)[...] = state
    steps = share(state_view, "s", quarter, 1, ((*far, shift * (1 - core)), (*near, shift * core)))
    next(steps)
    for i, (name, h) in enumerate((("or", left_m), ("ol", right_m), ("oo", opp_m))):
        arrived(name, wo_half(h, core))
        send("os%d" % i, wo_half(h, core), wo_half(h, core), sibling)
    counts(1)
    counts(2)
    next(steps)
    counts(3)
    next(steps)

    next(steps)

    scale = LOG2_E * head_width ** -0.5
    for j in range(3):
        loads["w%d" % j].wait()

    def project(slot):
        rows = pl.ds(pl.multiple_of(slot * nodes, 128), nodes)
        if isinstance(slot, int):
            query[...] = (nn(st[rows, :], wqkv[:, :head_width]) * scale).astype(BF16)
        kv[...] = nn(st[rows, :], wqkv[:, head_width:]).astype(BF16)

    def attend(slot, first):
        project(slot)
        cols = pl.ds(pl.multiple_of(slot * nodes, 128), nodes)
        masked = nt(query[...], kv[:, :head_width]) + bias[:, cols]
        new = jnp.max(masked, axis=-1, keepdims=True)
        if not first:
            new = jnp.maximum(new, top[...])
            old = jnp.exp2(top[...] - new)
        power = jnp.exp2(masked - new)
        count = jnp.sum(power, axis=-1, keepdims=True)
        summed = nn(power.astype(BF16), kv[:, head_width:])
        norm[...] = count if first else norm[...] * old + count
        acc[...] = summed if first else acc[...] * old + summed
        top[...] = new

    attend(1, True)
    all_passed(state_view, "su", 2 - 2 * core, quarter, shift * (1 - core))
    attend(2 - 2 * core, False)
    all_passed(state_view, "su", 2 * core, quarter, shift * core)
    attend(2 * core, False)

    def mixed_view(slot, h, start, size):
        cols = pl.ds(pl.multiple_of(h * head_width, 128), head_width)
        return mixed.at[pl.ds(slot * nodes + start, size), cols]

    mixed_view(0, m, 0, nodes)[...] = (acc[...] / norm[...]).astype(BF16)
    steps = share(mixed_view, "m", nodes, 0, (("md", 1, down, 0),))
    next(steps)

    loads["wo"].wait()
    for i, h in enumerate((left_m, right_m, opp_m)):
        arrived("os%d" % i, wo_half(h, 1 - core))
    loads["wdec"].wait()
    wod[...] = nn(wo[...].reshape(heads * head_width, width), wdec[...]).astype(BF16)
    from_state[...] = nn(st[nodes:, :], wdec[...])

    wdec_t[...] = jnp.transpose(wdec[...].astype(F32)).astype(BF16)
    e2[...] = nn(wdec_t[...], embed[...])
    next(steps)
    next(steps)
    next(steps)

    def decoded(slot):
        rows = pl.ds(slot * nodes, nodes)
        return jnp.transpose(nn(mixed[rows, :], wod[...]) + from_state[rows, :]).astype(BF16)

    e2[...] += nn(decoded(0), onehot[pl.ds(0, nodes), :])
    loads["whead"].wait()
    sent()
    all_passed(mixed_view, "md", 1, nodes)
    last_t[...] = decoded(1)
    block = points
    for i in range(points // block):
        cols = slice(i * block, (i + 1) * block)
        z = e2[:, cols] + nn(last_t[...], onehot[nodes:, cols])
        out_ref[:, cols] = nn(whead[...], silu(z).astype(BF16))

    sent()


def on_device(grid_state, targets, neighbours, w_in, b_in, mesh_gain, w_qkv, w_out, w_dec, w_head):
    points, channels = grid_state.shape
    nodes, nbr = neighbours.shape
    width = w_in.shape[1]
    quarter = nodes // 4
    half = quarter // 2
    span = 3 * nodes
    heads = 4
    head_width = w_qkv.shape[2]
    out_width = w_head.shape[1]
    regions = lax.axis_size("region")
    vmem = pl.BlockSpec(memory_space=pltpu.VMEM)
    anyw = pl.BlockSpec(memory_space=pl.ANY)
    V = pltpu.VMEM
    out = pl.pallas_call(
        functools.partial(kernel, regions),
        out_shape=pltpu.VMEM((out_width, points), F32),
        in_specs=[anyw] * 10,
        out_specs=vmem,
        scratch_shapes=[
            V((channels, points), BF16), V((1, points), jnp.int32), V((nbr, nodes), jnp.int32), V((channels, width), BF16),
            V((1, width), F32), V((1, width), F32),
            V((width, channels), BF16), V((width, 128), F32), V((width, 3 * head_width), BF16),
            V((heads, head_width, width), BF16), V((width, width), BF16), V((width, width), BF16),
            V((out_width, width), BF16),
            V((1, points), jnp.int32), V((nodes, nbr), jnp.int32),
            V((nodes // 8, 8 * nbr), jnp.int32), V((nodes // 8, 8 * nbr), jnp.int32),
            V((2 * nodes, points), BF16), V((width, points), BF16), V((width, points), F32),
            V((nodes, width), BF16), V((nodes, width), BF16), V((nodes, width), F32),
            V((quarter, width), BF16), V((half, width), BF16), V((half, width), BF16),
            V((2, quarter, width), BF16), V((quarter, width), BF16), V((quarter, width), BF16),
            V((span, width), BF16), V((nodes, head_width), BF16), V((nodes, 2 * head_width), BF16),
            V((nodes, span), F32), V((nodes, head_width), F32), V((nodes, 1), F32), V((nodes, 1), F32),
            V((2 * nodes, heads * head_width), BF16), V((heads * head_width, width), BF16),
            V((2 * nodes, width), F32), V((width, nodes), BF16),
            pltpu.SemaphoreType.DMA((len(NAMES),)), pltpu.SemaphoreType.DMA((len(NAMES),)),
            pltpu.SemaphoreType.DMA((12,)),
        ],
        compiler_params=pltpu.CompilerParams(
            collective_id=0, has_side_effects=True, vmem_limit_bytes=56 * 1024 * 1024
        ),
        cost_estimate=pl.CostEstimate(flops=10 * 10 ** 9, bytes_accessed=4 * 10 ** 6, transcendentals=3 * 10 ** 6),
    )(
        grid_state.T, targets.reshape(1, points), neighbours.T, w_in, b_in.reshape(1, width),
        mesh_gain.reshape(1, width), w_qkv, w_out, w_dec, w_head.T,
    )
    return out.T


def solution(mesh):
    placed = (
        P(("region", "mp"), None),
        P(("region", "mp")),
        P("region", None),
        P(),
        P(),
        P(),
        P(None, None, "mp"),
        P("mp", None),
        P(),
        P(),
    )
    return jax.shard_map(
        on_device, mesh=mesh, in_specs=placed, out_specs=P(("region", "mp"), None), check_vma=False
    )
```

```python
import functools

import jax
import jax.numpy as jnp
from jax import lax
from jax.experimental import pallas as pl
from jax.experimental.pallas import tpu as pltpu
from jax.sharding import PartitionSpec as P

MESH = pl.DeviceIdType.MESH
BF16 = jnp.bfloat16
F32 = jnp.float32
LOG2_E = 1.4426950408889634
ABSENT = -1e30

NAMES = (
    *("or", "ol", "oo", "os0", "os1", "os2"),
    *("n0", "n1", "n2", "n3"),
    *("ar", "al", "br0", "br1", "bl0", "bl1"),
    *("sr0", "sr1", "sl0", "sl1", "sf0", "sf1"),
    *("su0", "su1", "su2", "su3", "su4", "su5", "su6"),
    *("sd0", "sd1", "sd2", "sd3", "sd4", "sd5", "sd6"),
    *("mr0", "mr1", "ml0", "ml1", "mf0", "mf1"),
    *("md0", "md1", "md2", "md3", "md4", "md5", "md6"),
)
INDEX = {name: i for i, name in enumerate(NAMES)}


def nt(a, b):
    return lax.dot_general(a, b, (((1,), (1,)), ((), ())), preferred_element_type=F32)


def nn(a, b):
    return jnp.dot(a, b, preferred_element_type=F32)


def silu(z):
    half = 0.5 * z
    return half + half * jnp.tanh(half)


def kernel(
    regions,
    x_hbm, targets_hbm, nbr_hbm, w_in_hbm, b_hbm, gain_hbm, wqkv_hbm, wo_hbm, wdec_hbm, whead_hbm,
    out_ref,
    x, targets, nbr, w_in, b_in, gain, w_in_t, b_t, wqkv, wo, wdec, wdec_t, whead,
    rel, slots, code_hi, code_lo, onehot, embed, e2,
    send_n, recv_n, part, ra, ra_l, ra_r, rb, rb_l, rb_r,
    st, query, kv, bias, acc, top, norm, mixed, wod, from_state, last_t,
    ssem, rsem, lsem,
):
    r = lax.axis_index("region")
    m = lax.axis_index("mp")
    mps = 4
    up = (lax.rem(r + 1, regions), m)
    down = (lax.rem(r + regions - 1, regions), m)
    right_m = lax.rem(m + 1, mps)
    left_m = lax.rem(m + mps - 1, mps)
    opp_m = lax.rem(m + 2, mps)
    opposite = (r, opp_m)
    right = (r, right_m)
    left = (r, left_m)
    core = lax.rem(r, 2)
    sibling = (r + 1 - 2 * core, m)

    points = x.shape[1]
    width = embed.shape[0]
    nodes = nbr.shape[1]
    quarter = nodes // 4
    half = quarter // 2
    span = 3 * nodes
    neighbours = slots.shape[1]
    heads, head_width = wo.shape[0], wo.shape[1]

    started = []

    def send(name, src, dst, dev, shift=0):
        i = INDEX[name] + shift
        c = pltpu.make_async_remote_copy(
            src_ref=src, dst_ref=dst, send_sem=ssem.at[i], recv_sem=rsem.at[i],
            device_id=dev, device_id_type=MESH,
        )
        c.start()
        started.append(c)

    def sent():
        for c in started:
            c.wait_send()
        started.clear()

    def arrived(name, dst, shift=0):
        i = INDEX[name] + shift
        pltpu.make_async_remote_copy(
            src_ref=dst, dst_ref=dst, send_sem=ssem.at[i], recv_sem=rsem.at[i],
            device_id=right, device_id_type=MESH,
        ).wait_recv()

    loads = {}
    for i, (name, src, dst) in enumerate((
        ("w_in", w_in_hbm, w_in), ("x", x_hbm, x), ("b", b_hbm, b_in), ("targets", targets_hbm, targets), ("gain", gain_hbm, gain), ("wo", wo_hbm, wo.at[m]), ("wdec", wdec_hbm, wdec), ("whead", whead_hbm, whead), ("nbr", nbr_hbm, nbr),
        *(("w%d" % j, wqkv_hbm.at[j], wqkv.at[:, pl.ds(j * head_width, head_width)]) for j in range(3)),
    )):
        loads[name] = pltpu.make_async_copy(src, dst, lsem.at[i])
        loads[name].start()

    barrier = pltpu.get_barrier_semaphore()
    for dev in (up, down, right, left, opposite):
        pl.semaphore_signal(barrier, inc=1, device_id=dev, device_id_type=MESH)

    here = r * nodes
    total = regions * nodes
    loads["w_in"].wait()
    w_in_t[...] = jnp.transpose(w_in[...].astype(F32)).astype(BF16)
    loads["b"].wait()
    b_t[...] = jnp.transpose(jnp.broadcast_to(b_in[...], (128, width)))
    loads["targets"].wait()
    t = targets[...] - here
    rel[...] = jnp.where(t < 0, t + total, t)

    loads["x"].wait()
    z = nn(w_in_t[...], x[...]) + jnp.concatenate([b_t[...]] * (points // 128), axis=1)
    embed[...] = silu(z).astype(BF16)

    pl.semaphore_wait(barrier, 5)

    ho = head_width // 2

    def wo_half(h, which):
        return wo.at[h, pl.ds(pl.multiple_of(which * ho, 16), ho), :]

    for name, dev in (("or", right), ("ol", left), ("oo", opposite)):
        send(name, wo_hbm.at[pl.ds(pl.multiple_of(core * ho, 16), ho), :], wo_half(m, core), dev)

    order = (opp_m, right_m, left_m, m)

    def rows_of(ref, q, start=0, size=quarter, slot=0):
        return ref.at[pl.ds(pl.multiple_of(slot * nodes + q * quarter + start, 16), size)]

    def sums(slot, quarters):
        picks = []
        for q in quarters:
            first = slot * nodes + q * quarter
            ids = lax.broadcasted_iota(jnp.int32, (quarter, points), 0) + first
            picks.append((ids == rel[...]).astype(F32).astype(BF16))
            rows_of(onehot, q, slot=slot)[...] = picks[-1]
        return nt(jnp.concatenate(picks, axis=0), embed[...])

    for k in (0, 2):
        rows_of(send_n, k, 0, 2 * quarter)[...] = sums(1, order[k:k + 2]).astype(BF16)
        for i in (k, k + 1):
            send("n%d" % i, rows_of(send_n, i), rows_of(recv_n, i), up)
    part[...] = sums(0, order)

    def both(q, start=0, size=quarter):
        return rows_of(part, q, start, size)[...] + rows_of(recv_n, q, start, size)[...].astype(F32)

    lo, hi = pl.ds(0, half), pl.ds(half, half)
    arrived("n0", rows_of(recv_n, 0))
    ra[...] = both(0).astype(BF16)
    send("ar", ra.at[lo], ra_l, right)
    send("al", ra.at[hi], ra_r, left)

    loads["nbr"].wait()
    s = jnp.transpose(nbr[...]) - (here - nodes)
    s = jnp.where(s < 0, s + total, s)
    slots[...] = jnp.where(s >= total, s - total, s)
    groups = nodes // 8
    for i in range(8):
        piece = slots[pl.ds(i, groups, stride=8), :]
        cols = slice(i * neighbours, (i + 1) * neighbours)
        code_hi[:, cols] = (piece >> 7) + i * 16
        code_lo[:, cols] = piece & 127
    together = 5 if groups % 20 == 0 else 4
    share_of_counts = groups // (4 * together)

    def count_groups(j, _):
        ids = lax.broadcasted_iota(jnp.int32, (128, 8 * neighbours), 0)
        for u in range(together):
            g = j * together + u
            high = (ids == code_hi[pl.ds(g, 1), :]).astype(F32).astype(BF16)
            low = (ids == code_lo[pl.ds(g, 1), :]).astype(F32).astype(BF16)
            count = nt(high, low)
            log = jnp.where(count > 0.0, jnp.log2(count), ABSENT).reshape(8, 16, 128)
            for c in range(span // 128):
                bias[pl.ds(pl.multiple_of(g * 8, 8), 8), c * 128:(c + 1) * 128] = log[:, c, :]
        return 0

    def counts(i):
        lax.fori_loop(i * share_of_counts, (i + 1) * share_of_counts, count_groups, 0)


    counts(0)
    arrived("n1", rows_of(recv_n, 1))
    rb[0, hi] = both(1, half, half).astype(BF16)
    send("br1", rb.at[0, hi], rb_l.at[hi], right)
    arrived("ar", ra_l)
    rb[0, lo] = (both(1, 0, half) + ra_l[...].astype(F32)).astype(BF16)
    send("br0", rb.at[0, lo], rb_l.at[lo], right)
    arrived("n2", rows_of(recv_n, 2))
    rb[1, lo] = both(2, 0, half).astype(BF16)
    send("bl0", rb.at[1, lo], rb_r.at[lo], left)
    arrived("al", ra_r)
    rb[1, hi] = (both(2, half, half) + ra_r[...].astype(F32)).astype(BF16)
    send("bl1", rb.at[1, hi], rb_r.at[hi], left)
    arrived("n3", rows_of(recv_n, 3))
    for name, ref in (("br1", rb_l.at[hi]), ("br0", rb_l.at[lo]), ("bl0", rb_r.at[lo]), ("bl1", rb_r.at[hi])):
        arrived(name, ref)
    mesh_in = both(3) + rb_l[...].astype(F32) + rb_r[...].astype(F32)
    loads["gain"].wait()
    mean = jnp.mean(mesh_in * mesh_in, axis=-1, keepdims=True)
    state = (mesh_in * lax.rsqrt(mean + 1e-05) * gain[...]).astype(BF16)

    def share(view, tag, size, slot, out):
        cut = size // 2

        def give(name, q, start, dev):
            send(tag + name, view(slot, q, start, cut), view(slot, q, start, cut), dev)

        def got(name, q, start):
            arrived(tag + name, view(slot, q, start, cut))

        def pass_on(i, q, start=0, count=cut):
            for name, to_slot, dev, shift in out:
                send(name + str(i), view(slot, q, start, count), view(to_slot, q, start, count), dev, shift)

        give("r0", m, 0, right)
        yield
        give("l1", m, cut, left)
        pass_on(0, m, 0, size)
        give("r1", m, cut, right)
        give("l0", m, 0, left)
        yield
        got("r0", left_m, 0)
        give("f0", left_m, 0, right)
        pass_on(1, left_m)
        got("l1", right_m, cut)
        give("f1", right_m, cut, left)
        pass_on(2, right_m, cut)
        yield
        got("r1", left_m, cut)
        pass_on(3, left_m, cut)
        got("l0", right_m, 0)
        pass_on(4, right_m)
        yield
        got("f0", opp_m, 0)
        pass_on(5, opp_m)
        got("f1", opp_m, cut)
        pass_on(6, opp_m, cut)
        yield

    def all_passed(view, name, slot, size, shift=0):
        for i in range(7):
            arrived(name + str(i), view(slot, 0, 0, size // 2 if i else size), shift)

    def state_view(slot, q, start, size):
        return rows_of(st, q, start, size, slot)

    shift = INDEX["sd0"] - INDEX["su0"]
    far = "su", 2 - 2 * core, (lax.rem(r + regions - 1 + 2 * core, regions), m)
    near = "su", 2 * core, sibling
    state_view(1, m, 0, quarter)[...] = state
    steps = share(state_view, "s", quarter, 1, ((*far, shift * (1 - core)), (*near, shift * core)))
    next(steps)
    next(steps)
    for i, (name, h) in enumerate((("or", left_m), ("ol", right_m), ("oo", opp_m))):
        arrived(name, wo_half(h, core))
        send("os%d" % i, wo_half(h, core), wo_half(h, core), sibling)
    counts(1)
    counts(2)
    next(steps)
    counts(3)
    next(steps)

    next(steps)

    scale = LOG2_E * head_width ** -0.5
    for j in range(3):
        loads["w%d" % j].wait()

    def project(slot):
        rows = pl.ds(pl.multiple_of(slot * nodes, 128), nodes)
        if isinstance(slot, int):
            query[...] = (nn(st[rows, :], wqkv[:, :head_width]) * scale).astype(BF16)
        kv[...] = nn(st[rows, :], wqkv[:, head_width:]).astype(BF16)

    def attend(slot, first, at=slice(None), projected=False):
        if not projected:
            project(slot)
        cols = pl.ds(pl.multiple_of(slot * nodes, 128), nodes)
        masked = nt(query[at], kv[:, :head_width]) + bias[at, cols]
        new = jnp.max(masked, axis=-1, keepdims=True)
        if not first:
            new = jnp.maximum(new, top[at])
            old = jnp.exp2(top[at] - new)
        power = jnp.exp2(masked - new)
        count = jnp.sum(power, axis=-1, keepdims=True)
        summed = nn(power.astype(BF16), kv[:, head_width:])
        norm[at] = count if first else norm[at] * old + count
        acc[at] = summed if first else acc[at] * old + summed
        top[at] = new

    attend(1, True)
    all_passed(state_view, "su", 2 - 2 * core, quarter, shift * (1 - core))
    attend(2 - 2 * core, False)
    all_passed(state_view, "su", 2 * core, quarter, shift * core)

    def mixed_view(slot, h, start, size):
        cols = pl.ds(pl.multiple_of(h * head_width, 128), head_width)
        return mixed.at[pl.ds(slot * nodes + start, size), cols]

    steps = share(mixed_view, "m", nodes, 0, (("md", 1, down, 0),))
    for first in (0, nodes // 2):
        at = slice(first, first + nodes // 2)
        attend(2 * core, False, at, first > 0)
        mixed_view(0, m, first, nodes // 2)[...] = (acc[at] / norm[at]).astype(BF16)
        next(steps)

    loads["wo"].wait()
    for i, h in enumerate((left_m, right_m, opp_m)):
        arrived("os%d" % i, wo_half(h, 1 - core))
    loads["wdec"].wait()
    wod[...] = nn(wo[...].reshape(heads * head_width, width), wdec[...]).astype(BF16)
    from_state[...] = nn(st[nodes:, :], wdec[...])

    wdec_t[...] = jnp.transpose(wdec[...].astype(F32)).astype(BF16)
    e2[...] = nn(wdec_t[...], embed[...])
    next(steps)
    next(steps)
    next(steps)

    def decoded(slot):
        rows = pl.ds(slot * nodes, nodes)
        return jnp.transpose(nn(mixed[rows, :], wod[...]) + from_state[rows, :]).astype(BF16)

    e2[...] += nn(decoded(0), onehot[pl.ds(0, nodes), :])
    loads["whead"].wait()
    sent()
    all_passed(mixed_view, "md", 1, nodes)
    last_t[...] = decoded(1)
    block = points
    for i in range(points // block):
        cols = slice(i * block, (i + 1) * block)
        z = e2[:, cols] + nn(last_t[...], onehot[nodes:, cols])
        out_ref[:, cols] = nn(whead[...], silu(z).astype(BF16))

    sent()


def on_device(grid_state, targets, neighbours, w_in, b_in, mesh_gain, w_qkv, w_out, w_dec, w_head):
    points, channels = grid_state.shape
    nodes, nbr = neighbours.shape
    width = w_in.shape[1]
    quarter = nodes // 4
    half = quarter // 2
    span = 3 * nodes
    heads = 4
    head_width = w_qkv.shape[2]
    out_width = w_head.shape[1]
    regions = lax.axis_size("region")
    vmem = pl.BlockSpec(memory_space=pltpu.VMEM)
    anyw = pl.BlockSpec(memory_space=pl.ANY)
    V = pltpu.VMEM
    out = pl.pallas_call(
        functools.partial(kernel, regions),
        out_shape=pltpu.VMEM((out_width, points), F32),
        in_specs=[anyw] * 10,
        out_specs=vmem,
        scratch_shapes=[
            V((channels, points), BF16), V((1, points), jnp.int32), V((nbr, nodes), jnp.int32), V((channels, width), BF16),
            V((1, width), F32), V((1, width), F32),
            V((width, channels), BF16), V((width, 128), F32), V((width, 3 * head_width), BF16),
            V((heads, head_width, width), BF16), V((width, width), BF16), V((width, width), BF16),
            V((out_width, width), BF16),
            V((1, points), jnp.int32), V((nodes, nbr), jnp.int32),
            V((nodes // 8, 8 * nbr), jnp.int32), V((nodes // 8, 8 * nbr), jnp.int32),
            V((2 * nodes, points), BF16), V((width, points), BF16), V((width, points), F32),
            V((nodes, width), BF16), V((nodes, width), BF16), V((nodes, width), F32),
            V((quarter, width), BF16), V((half, width), BF16), V((half, width), BF16),
            V((2, quarter, width), BF16), V((quarter, width), BF16), V((quarter, width), BF16),
            V((span, width), BF16), V((nodes, head_width), BF16), V((nodes, 2 * head_width), BF16),
            V((nodes, span), F32), V((nodes, head_width), F32), V((nodes, 1), F32), V((nodes, 1), F32),
            V((2 * nodes, heads * head_width), BF16), V((heads * head_width, width), BF16),
            V((2 * nodes, width), F32), V((width, nodes), BF16),
            pltpu.SemaphoreType.DMA((len(NAMES),)), pltpu.SemaphoreType.DMA((len(NAMES),)),
            pltpu.SemaphoreType.DMA((12,)),
        ],
        compiler_params=pltpu.CompilerParams(
            collective_id=0, has_side_effects=True, vmem_limit_bytes=56 * 1024 * 1024
        ),
        cost_estimate=pl.CostEstimate(flops=10 * 10 ** 9, bytes_accessed=4 * 10 ** 6, transcendentals=3 * 10 ** 6),
    )(
        grid_state.T, targets.reshape(1, points), neighbours.T, w_in, b_in.reshape(1, width),
        mesh_gain.reshape(1, width), w_qkv, w_out, w_dec, w_head.T,
    )
    return out.T


def solution(mesh):
    placed = (
        P(("region", "mp"), None),
        P(("region", "mp")),
        P("region", None),
        P(),
        P(),
        P(),
        P(None, None, "mp"),
        P("mp", None),
        P(),
        P(),
    )
    return jax.shard_map(
        on_device, mesh=mesh, in_specs=placed, out_specs=P(("region", "mp"), None), check_vma=False
    )
```
